32 devices in a mesh: grp: 2 (over y), space: 4 (over z), snap: 4 (over x, core).
Axes of the slice: x: 2, y: 2, z: 4, core: 2. Of those that a mesh axis runs over, the one named last changes fastest.
Arguments:
- velocity: bfloat16 [32, 3, 8, 96, 128], P(('grp', 'snap'), None, None, 'space'), parts along dimension 0, may hold values from -20 to 20
- row_level: int32 [96], P('space'), may hold values from 0 to 127
- metric_table: float32 [8, 128], replicated, may hold values from 0.5 to 2
Outputs:
- gram: float32 [32, 16], P(('grp', 'snap')), parts along dimension 0
- profile: float32 [32, 96], P(('grp', 'snap'), 'space'), parts along dimension 0
The draws below stay inside these ranges and needn't reach their ends.
There are 2 independent parts, one for each index of `grp`. The reference program is written for one: setup_inputs(seed, part) draws one part's arguments, and reference() takes and returns one part's arrays. A program takes and returns all parts, laid end to end along the dimension named above; an argument that names none is the same for every part. Nothing has to cross between parts.
All inputs are finite; a program needn't handle non-finite values.
Results may differ from the reference program's by a relative error of at most 0.0005.
Values may be sent and summed in bfloat16 or wider, within the bound.
No kernel may reach another device: no remote copies, remote signals or barrier semaphores. Data moves between devices by JAX's collectives and lax.ppermute only.
A program may use at most 128 MiB of HBM per device.

```python
import math
import jax
import jax.numpy as jnp
from jax import lax

PLANES = 8
NZW = 128
LEVELS = 128
SNAPS = 16
NY = 96


def draw_velocity(key, part):
    key = jax.random.fold_in(key, 7)
    blend_key, motif_key, noise_key, amplitude_key, location_key, pulse_key = jax.random.split(key, 6)
    domain_extent = (SNAPS, 3, PLANES, NY, NZW)
    cells = (1, 1, PLANES, NY, NZW)
    level = jnp.exp(jax.random.uniform(amplitude_key, cells, jnp.float32, -1.2, 1.2))
    hotspot_positions = jax.random.bernoulli(location_key, 1.0 / 128.0, cells).astype(jnp.float32)
    mixing = jax.random.truncated_normal(blend_key, -3.0, 3.0, (SNAPS, 4), jnp.float32)
    patterns = 0.35 * jax.random.truncated_normal(motif_key, -3.0, 3.0, (4,) + domain_extent[1:], jnp.float32)
    jitter = 0.7 * jax.random.truncated_normal(noise_key, -3.0, 3.0, domain_extent, jnp.float32)
    pulse_amplitude = jax.random.truncated_normal(pulse_key, -1.5, 1.5, domain_extent, jnp.float32)
    summed_field = jitter * level
    for index in range(4):
        summed_field = summed_field + mixing[:, index][:, None, None, None, None] * patterns[index][None]
    summed_field = summed_field + 11.0 * hotspot_positions * pulse_amplitude
    return jnp.clip(summed_field, -20.0, 20.0).astype(jnp.bfloat16)


def touch_ends(drawn, own_key, smallest, high):
    place = [jax.random.randint(jax.random.fold_in(own_key, axis), (), 0, length) for axis, length in enumerate(drawn.shape)]
    widest = drawn.shape.index(max(drawn.shape))
    beside = place[:widest] + [(place[widest] + 1) % drawn.shape[widest]] + place[widest + 1:]
    return drawn.at[tuple(place)].set(smallest).at[tuple(beside)].set(high)


def setup_inputs(seed: int = 0, part: int = 0) -> dict:
    seeds = jax.random.split(jax.random.key(seed), 4)
    part_keys = jax.random.split(jax.random.fold_in(seeds[3], part), 4)
    return {
        "velocity": draw_velocity(jax.random.fold_in(jax.random.fold_in(seeds[3], part), 71), part),
        "row_level": touch_ends(jax.random.randint(seeds[1], (NY,), 0, LEVELS), jax.random.fold_in(seeds[1], 1), 0, LEVELS - 1).astype(jnp.int32),
        "metric_table": jnp.clip(jnp.exp(jax.random.uniform(seeds[2], (PLANES, LEVELS), jnp.float32, math.log(0.5), math.log(2.0))), 0.5, 2.0),
    }


def derivative(field, axis):
    count = field.shape[axis]
    first = lax.slice_in_dim(field, 1, 2, axis=axis) - lax.slice_in_dim(field, 0, 1, axis=axis)
    inner = (lax.slice_in_dim(field, 2, count, axis=axis) - lax.slice_in_dim(field, 0, count - 2, axis=axis)) * 0.5
    last = lax.slice_in_dim(field, count - 1, count, axis=axis) - lax.slice_in_dim(field, count - 2, count - 1, axis=axis)
    return jnp.concatenate([first, inner, last], axis=axis)


def features(padded, metric):
    field = padded.astype(jnp.float32)
    inner = field[:, :, :, 1:-1, :]
    normal_grad = (field[:, :, :, 2:, :] - field[:, :, :, :-2, :]) * 0.5 * metric[None, None, :, :, None]
    stream_grad = derivative(inner, 2)
    span_grad = derivative(inner, 4)
    joined = jnp.concatenate([inner, 0.5 * stream_grad, 0.5 * normal_grad, 0.5 * span_grad], axis=1)
    return joined.astype(jnp.bfloat16)


def weighted_copy(feats, volume):
    return (feats.astype(jnp.float32) * volume[None, None, :, :, None]).astype(jnp.bfloat16)


def reference(velocity, row_level, metric_table):
    snaps_all = velocity.shape[0]
    planes = velocity.shape[2]
    rows_all = velocity.shape[3]
    span_cells = velocity.shape[4]
    row_ids = jnp.arange(rows_all, dtype=jnp.int32)
    stretch = 0.25 + 2.25 * row_ids.astype(jnp.float32) / (rows_all - 1)
    picked = metric_table[:, row_level]
    metric = picked / stretch[None, :]
    volume = stretch[None, :] / picked
    padded = jnp.pad(velocity, ((0, 0), (0, 0), (0, 0), (1, 1), (0, 0)))

    def per_snapshot(single):
        feats = features(single[None], metric)
        weights = weighted_copy(feats, volume)
        energy = jnp.sum(weights.astype(jnp.float32) * feats.astype(jnp.float32), axis=(1, 2, 4)) / (planes * span_cells)
        return feats[0], weights[0], energy[0]

    feats_all, weights_all, profile = lax.map(per_snapshot, padded)
    gram = jnp.dot(weights_all.reshape(snaps_all, -1), feats_all.reshape(snaps_all, -1).T, preferred_element_type=jnp.float32)
    gram = gram * (1.0 / (planes * rows_all * span_cells))
    return gram, profile
```

```python
import functools

import jax
import jax.numpy as jnp
import numpy as np
from jax import lax
from jax.experimental import pallas as pl
from jax.experimental.pallas import tpu as pltpu
from jax.sharding import PartitionSpec as P

F32 = jnp.float32
BF16 = jnp.bfloat16
ROWS = 8
VMEM = pl.BlockSpec(memory_space=pltpu.VMEM)
SMEM = pl.BlockSpec(memory_space=pltpu.SMEM)
PARAMS = pltpu.CompilerParams(vmem_limit_bytes=16 * 2**20)


def span_operator(cells):
    diff = np.zeros((cells, cells), np.float32)
    for i in range(cells):
        lo, hi = max(i - 1, 0), min(i + 1, cells - 1)
        scale = 0.5 / (hi - lo)
        diff[i, hi] += scale
        diff[i, lo] -= scale
    return diff.T @ diff


def sublane(shape):
    return lax.broadcasted_iota(jnp.int32, shape, len(shape) - 2)


def lanes(shape):
    return lax.broadcasted_iota(jnp.int32, shape, len(shape) - 1)


def prep_kernel(place_ref, level_ref, table_ref, top_ref, bottom_ref, up_ref, down_ref, metric_ref, volume_ref):
    snaps, comps, planes, _, span = top_ref.shape
    rows = metric_ref.shape[1]
    levels = table_ref.shape[1]
    row = lax.broadcasted_iota(jnp.int32, (rows, levels), 0)
    level = jnp.zeros((rows, levels), jnp.int32)
    for j in range(rows):
        level = jnp.where(row == j, level_ref[j], level)
    chosen = level == lanes((rows, levels))
    row_ids = (place_ref[0] * rows + lax.broadcasted_iota(jnp.int32, (rows, span), 0)).astype(F32)
    stretch = 0.25 + 2.25 * row_ids / (place_ref[1] - 1).astype(F32)
    for p in range(planes):
        picked = jnp.sum(jnp.where(chosen, table_ref[p : p + 1, :], 0.0), axis=1, keepdims=True)
        picked = jnp.broadcast_to(picked, (rows, span))
        metric_ref[p] = picked / stretch
        volume_ref[p] = stretch / picked
    row8 = sublane((ROWS, span))
    for c in range(comps):
        for p in range(planes):
            up = jnp.zeros((ROWS, span), F32)
            down = jnp.zeros((ROWS, span), F32)
            for a in range(snaps):
                mine = row8 // 2 == a
                last = bottom_ref[a, c, p].astype(F32)
                first = top_ref[a, c, p].astype(F32)
                up = jnp.where(mine, pltpu.roll(last, (2 * a + 2) % ROWS, 0), up)
                down = jnp.where(mine, pltpu.roll(first, (2 * a) % ROWS, 0), down)
            up_ref[c * planes + p] = up.astype(BF16)
            down_ref[c * planes + p] = down.astype(BF16)
    count = comps * planes
    for ref, j in ((up_ref, rows - 1), (down_ref, 0)):
        rest = jnp.zeros((ROWS, span), F32)
        for p in range(planes):
            rest = jnp.where(row8 == p, jnp.broadcast_to(metric_ref[p, j : j + 1, :], (ROWS, span)), rest)
        for piece in range(3):
            part = rest.astype(BF16)
            ref[count + piece] = part
            rest = rest - part.astype(F32)


def weigh_kernel(u_ref, metric_ref, volume_ref, below_ref, above_ref, op_ref, w_ref, profile_ref, f_ref, e_ref, prof_ref):
    snaps, comps, planes, rows, span = u_ref.shape
    count = comps * planes
    m_below = sum(below_ref[count + i].astype(F32) for i in range(3)) * 0.0625
    m_above = sum(above_ref[count + i].astype(F32) for i in range(3)) * 0.0625
    first, end = ROWS, ROWS + rows
    for a in range(snaps):
        prof_ref[a] = jnp.zeros((rows, span), F32)

    def field(c, carry):
        for a in range(snaps):
            raw = u_ref[a, c]
            spanned = jnp.dot(raw.reshape(planes * rows, span), op_ref[...], preferred_element_type=F32)
            spanned = spanned.reshape(planes, rows, span)
            u = raw.astype(F32)
            for p in range(planes):
                f_ref[p, first:end, :] = u[p]
                f_ref[p, 0:ROWS, :] = pltpu.roll(below_ref[c * planes + p].astype(F32), (ROWS - 2 - 2 * a) % ROWS, 0)
                f_ref[p, end : end + ROWS, :] = pltpu.roll(above_ref[c * planes + p].astype(F32), (-2 * a) % ROWS, 0)
            stream = [None] * planes
            for i in range(planes):
                lo, hi = max(i - 1, 0), min(i + 1, planes - 1)
                scale = 0.25 / (hi - lo) ** 2
                edge = (volume_ref[i] * scale) * (u[hi] - u[lo])
                stream[hi] = edge if stream[hi] is None else stream[hi] + edge
                stream[lo] = -edge if stream[lo] is None else stream[lo] - edge
            total = prof_ref[a]
            for p in range(planes):
                jump = f_ref[p, first + 1 : end + 1, :] - f_ref[p, first - 1 : end - 1, :]
                edge = (metric_ref[p] * 0.0625) * jump
                e_ref[p, first:end, :] = edge
                e_ref[p, first - 1 : first, :] = m_below[p : p + 1, :] * (
                    f_ref[p, first : first + 1, :] - f_ref[p, first - 2 : first - 1, :]
                )
                e_ref[p, end : end + 1, :] = m_above[p : p + 1, :] * (
                    f_ref[p, end + 1 : end + 2, :] - f_ref[p, end - 1 : end, :]
                )
                partial = volume_ref[p] * (u[p] + spanned[p]) + stream[p]
                total = total + (u[p] * partial + edge * jump)
                normal = e_ref[p, first - 1 : end - 1, :] - e_ref[p, first + 1 : end + 1, :]
                w_ref[a, c, p] = (partial + normal).astype(BF16)
            prof_ref[a] = total
        return carry

    lax.fori_loop(0, comps, field, 0)
    ones = jnp.ones((ROWS, span), F32)
    for a in range(snaps):
        sums = lax.dot_general(
            ones, prof_ref[a], (((1,), (1,)), ((), ())), precision=lax.Precision.HIGHEST, preferred_element_type=F32
        )
        profile_ref[a : a + 1, :] = sums[0:1, :] * (1.0 / (planes * span))


def pair_sums(left_at, right_at, lefts, rights, comps, planes, pairs):
    def step(index, sums):
        c, p = index // planes, index % planes
        left = [left_at(i, c, p).astype(F32) for i in range(lefts)]
        right = [right_at(i, c, p).astype(F32) for i in range(rights)]
        out = list(sums)
        for t in range(0, left[0].shape[0], ROWS):
            for k, (i, j) in enumerate(pairs):
                out[k] = out[k] + left[i][t : t + ROWS] * right[j][t : t + ROWS]
        return tuple(out)

    zero = jnp.zeros((ROWS, 128), F32)
    return lax.fori_loop(0, comps * planes, step, tuple(zero for _ in pairs))


def totals(sums):
    tiles = []
    for start in range(0, len(sums), ROWS):
        tile = jnp.concatenate([jnp.sum(s, axis=0, keepdims=True) for s in sums[start : start + ROWS]], axis=0)
        tiles.append(jnp.broadcast_to(jnp.sum(tile, axis=1, keepdims=True), tile.shape))
    return tiles


def chip_kernel(place_ref, u_ref, w_ref, mate_ref, block_ref):
    snaps, comps, planes, _, span = u_ref.shape
    half = ROWS // snaps
    pairs = [(j, i) for j in range(2 * snaps) for i in range(snaps)]
    pair_list = [(j, i) for j, i in pairs]

    def left(i, c, p):
        return w_ref[i, c, p] if i < snaps else mate_ref[i - snaps, c, p]

    sums = pair_sums(left, lambda i, c, p: u_ref[i, c, p], 2 * snaps, snaps, comps, planes, pair_list)
    tiles = totals(sums)
    lane, row = lanes((ROWS, span)), sublane((ROWS, span))
    block = jnp.zeros((ROWS, span), F32)
    for k, tile in enumerate(tiles):
        j = k * half + row // snaps
        column = jnp.where(j < snaps, place_ref[2] + j, place_ref[3] + j - snaps)
        block = block + jnp.where(lane == column, tile, 0.0)
    fold = block
    for i in range(1, half):
        fold = fold + pltpu.roll(block, i * snaps, 0)
    block_ref[...] = fold


def cross_kernel(chips, place_ref, *refs):
    starts, got = refs[0], refs[1 : chips]
    w_ref, mate_ref, block_ref = refs[chips : chips + 3]
    own_ref, mate_out = refs[chips + 3 : chips + 5]
    back = refs[chips + 5 :]
    snaps, comps, planes, _, span = got[0].shape
    half = ROWS // snaps
    lane, row = lanes((ROWS, span)), sublane((ROWS, span))
    own = block_ref[...]
    mate = jnp.zeros((ROWS, span), F32)
    for k in range(chips - 1):
        start = starts[2 * k]
        column = starts[2 * k + 1]

        def left(i, c, p):
            return w_ref[i, c, start + p] if i < snaps else mate_ref[i - snaps, c, start + p]

        pairs = [(i, j) for i in range(2 * snaps) for j in range(snaps)]
        sums = pair_sums(left, lambda i, c, p: got[k][i, c, p], 2 * snaps, snaps, comps, planes, pairs)
        block = jnp.zeros((ROWS, span), F32)
        for t, tile in enumerate(totals(sums)):
            i = t * half + row // snaps
            to = jnp.where(i < snaps, place_ref[2] + i, place_ref[3] + i - snaps)
            block = block + jnp.where(lane == to, tile, 0.0)
        fold = block
        for i in range(1, half):
            fold = fold + pltpu.roll(block, i * snaps, 0)
        back[k][...] = fold
        flipped = [sums[i * snaps + j] for j in range(snaps) for i in range(2 * snaps)]
        for t, tile in enumerate(totals(flipped)):
            own = own + jnp.where((lane == column + t) & (row < snaps), tile, 0.0)
            mate = mate + jnp.where((lane == column + t) & (row >= snaps), tile, 0.0)
    own_ref[...] = own
    mate_out[...] = pltpu.roll(mate, ROWS - snaps, 0)


def local(velocity, row_level, metric_table):
    snaps, comps, planes, rows, span = velocity.shape
    spaces, cores = lax.axis_size("space"), lax.axis_size("snap")
    chips = cores // 2
    z, s = lax.axis_index("space"), lax.axis_index("snap")
    chip, core = s // 2, s % 2
    mate = s + 1 - 2 * core
    half = planes // 2
    place = jnp.stack([z, jnp.int32(rows * spaces), s * snaps, mate * snaps]).astype(jnp.int32)

    def begin(worker, other):
        return jnp.where(worker < other, 0, half).astype(jnp.int32)

    got = []
    for k in range(1, chips):
        start = begin((chip + k) % chips, chip)
        piece = lax.dynamic_slice_in_dim(velocity, start, half, axis=2)
        got.append(lax.ppermute(piece, "snap", [(i, (i + 2 * k) % cores) for i in range(cores)]))

    up, down, metric, volume = pl.pallas_call(
        prep_kernel,
        name="prep",
        grid=(1,),
        out_shape=[
            jax.ShapeDtypeStruct((comps * planes + 3, ROWS, span), BF16),
            jax.ShapeDtypeStruct((comps * planes + 3, ROWS, span), BF16),
            jax.ShapeDtypeStruct((planes, rows, span), F32),
            jax.ShapeDtypeStruct((planes, rows, span), F32),
        ],
        in_specs=[
            SMEM,
            SMEM,
            VMEM,
            pl.BlockSpec((snaps, comps, planes, ROWS, span), lambda i: (0, 0, 0, 0, 0)),
            pl.BlockSpec((snaps, comps, planes, ROWS, span), lambda i: (0, 0, 0, rows // ROWS - 1, 0)),
        ],
        out_specs=[VMEM] * 4,
        compiler_params=PARAMS,
    )(place, row_level, metric_table, velocity, velocity)
    below = lax.ppermute(up, "space", [(i, i + 1) for i in range(spaces - 1)])
    above = lax.ppermute(down, "space", [(i + 1, i) for i in range(spaces - 1)])

    operator = jnp.asarray(span_operator(span), BF16)
    w, profile = pl.pallas_call(
        weigh_kernel,
        name="weigh",
        out_shape=[
            jax.ShapeDtypeStruct(velocity.shape, BF16),
            jax.ShapeDtypeStruct((snaps, rows), F32),
        ],
        in_specs=[VMEM] * 6,
        out_specs=[VMEM] * 2,
        scratch_shapes=[
            pltpu.VMEM((planes, rows + 2 * ROWS, span), F32),
            pltpu.VMEM((planes, rows + 2 * ROWS, span), F32),
            pltpu.VMEM((snaps, rows, span), F32),
        ],
        compiler_params=PARAMS,
    )(velocity, metric, volume, below, above, operator)
    w_mate = lax.ppermute(w, "snap", [(i, i ^ 1) for i in range(cores)])
    tile = jax.ShapeDtypeStruct((ROWS, span), F32)
    block = pl.pallas_call(
        chip_kernel,
        name="chip",
        out_shape=tile,
        in_specs=[SMEM] + [VMEM] * 3,
        out_specs=VMEM,
        compiler_params=PARAMS,
    )(place, velocity, w, w_mate)

    starts = []
    for k in range(1, chips):
        source = (chip - k) % chips
        starts += [begin(chip, source), (2 * source + core) * snaps]
    own, for_mate, *back = pl.pallas_call(
        functools.partial(cross_kernel, chips),
        name="cross",
        out_shape=[tile] * (chips + 1),
        in_specs=[SMEM, SMEM] + [VMEM] * (chips + 2),
        out_specs=[VMEM] * (chips + 1),
        compiler_params=PARAMS,
    )(place, jnp.stack(starts).astype(jnp.int32), *got, w, w_mate, block)
    total = own
    for k in range(1, chips):
        total = total + lax.ppermute(back[k - 1], "snap", [(i, (i - 2 * k) % cores) for i in range(cores)])
    total = total + lax.ppermute(for_mate, "snap", [(i, i ^ 1) for i in range(cores)])
    gram = total
    for k in range(1, spaces):
        gram = gram + lax.ppermute(total, "space", [(i, (i + k) % spaces) for i in range(spaces)])
    gram = gram[:snaps, : snaps * cores] * (1.0 / (planes * rows * spaces * span))
    return gram, profile


def solution(mesh):
    in_specs = (P(("grp", "snap"), None, None, "space", None), P("space"), P())
    out_specs = (P(("grp", "snap"), None), P(("grp", "snap"), "space"))
    return jax.shard_map(local, mesh=mesh, in_specs=in_specs, out_specs=out_specs, check_vma=False)
```

```python
import functools

import jax
import jax.numpy as jnp
import numpy as np
from jax import lax
from jax.experimental import pallas as pl
from jax.experimental.pallas import tpu as pltpu
from jax.sharding import PartitionSpec as P

F32 = jnp.float32
BF16 = jnp.bfloat16
ROWS = 8
VMEM = pl.BlockSpec(memory_space=pltpu.VMEM)
SMEM = pl.BlockSpec(memory_space=pltpu.SMEM)


def call(kernel, name, out_shape, in_specs, scratch_shapes=()):
    single = not isinstance(out_shape, list)
    return pl.pallas_call(
        kernel,
        name=name,
        out_shape=out_shape,
        in_specs=in_specs,
        out_specs=VMEM if single else [VMEM] * len(out_shape),
        scratch_shapes=list(scratch_shapes),
        compiler_params=pltpu.CompilerParams(vmem_limit_bytes=16 * 2**20),
        cost_estimate=pl.CostEstimate(flops=1000, bytes_accessed=1000, transcendentals=0),
    )


def span_operator(cells):
    diff = np.zeros((cells, cells), np.float32)
    for i in range(cells):
        lo, hi = max(i - 1, 0), min(i + 1, cells - 1)
        scale = 0.5 / (hi - lo)
        diff[i, hi] += scale
        diff[i, lo] -= scale
    return diff.T @ diff


def sublane(shape):
    return lax.broadcasted_iota(jnp.int32, shape, len(shape) - 2)


def lanes(shape):
    return lax.broadcasted_iota(jnp.int32, shape, len(shape) - 1)


def pack_kernel(u_ref, metric_ref, up_ref, down_ref):
    snaps, comps, planes, rows, span = u_ref.shape
    count = comps * planes
    row8 = sublane((ROWS, span))
    for ref, j in ((up_ref, rows - 1), (down_ref, 0)):
        rest = jnp.zeros((ROWS, span), F32)
        for p in range(planes):
            rest = jnp.where(row8 == p, jnp.broadcast_to(metric_ref[p, j : j + 1, :], (ROWS, span)), rest)
        for piece in range(3):
            part = rest.astype(BF16)
            ref[count + piece] = part
            rest = rest - part.astype(F32)
    for c in range(comps):
        for p in range(planes):
            up = jnp.zeros((ROWS, span), F32)
            down = jnp.zeros((ROWS, span), F32)
            for a in range(snaps):
                mine = row8 // 2 == a
                first = u_ref[a, c, p, 0:ROWS, :].astype(F32)
                last = u_ref[a, c, p, rows - ROWS : rows, :].astype(F32)
                up = jnp.where(mine, pltpu.roll(last, (2 * a + 2) % ROWS, 0), up)
                down = jnp.where(mine, pltpu.roll(first, (2 * a) % ROWS, 0), down)
            up_ref[c * planes + p] = up.astype(BF16)
            down_ref[c * planes + p] = down.astype(BF16)


def inner_kernel(u_ref, metric_ref, volume_ref, op_ref, part_ref, energy_ref, f_ref, e_ref):
    snaps, comps, planes, rows, span = u_ref.shape
    first, end = ROWS, ROWS + rows
    row = sublane((rows, span))
    within = (row > 0) & (row < rows - 1)
    for a in range(snaps):
        energy_ref[a] = jnp.zeros((rows, span), F32)
    for p in range(planes):
        f_ref[p, 0:first, :] = jnp.zeros((ROWS, span), F32)
        f_ref[p, end : end + ROWS, :] = jnp.zeros((ROWS, span), F32)
        e_ref[p, 0:first, :] = jnp.zeros((ROWS, span), F32)
        e_ref[p, end : end + ROWS, :] = jnp.zeros((ROWS, span), F32)

    def field(c, carry):
        for a in range(snaps):
            raw = u_ref[a, c]
            spanned = jnp.dot(raw.reshape(planes * rows, span), op_ref[...], preferred_element_type=F32)
            spanned = spanned.reshape(planes, rows, span)
            u = raw.astype(F32)
            for p in range(planes):
                f_ref[p, first:end, :] = u[p]
            stream = [None] * planes
            for i in range(planes):
                lo, hi = max(i - 1, 0), min(i + 1, planes - 1)
                scale = 0.25 / (hi - lo) ** 2
                edge = (volume_ref[i] * scale) * (u[hi] - u[lo])
                stream[hi] = edge if stream[hi] is None else stream[hi] + edge
                stream[lo] = -edge if stream[lo] is None else stream[lo] - edge
            total = energy_ref[a]
            for p in range(planes):
                jump = f_ref[p, first + 1 : end + 1, :] - f_ref[p, first - 1 : end - 1, :]
                edge = jnp.where(within, (metric_ref[p] * 0.0625) * jump, 0.0)
                e_ref[p, first:end, :] = edge
                partial = volume_ref[p] * (u[p] + spanned[p]) + stream[p]
                total = total + (u[p] * partial + edge * jump)
                normal = e_ref[p, first - 1 : end - 1, :] - e_ref[p, first + 1 : end + 1, :]
                part_ref[a, c, p] = partial + normal
            energy_ref[a] = total
        return carry

    lax.fori_loop(0, comps, field, 0)


def edge_kernel(place_ref, u_ref, part_ref, metric_ref, low_ref, high_ref, here_ref, other_ref, gain_ref, below_ref, above_ref):
    snaps, comps, planes, rows, span = u_ref.shape
    count = comps * planes
    half = planes // 2
    row8 = sublane((ROWS, span))
    below_ref[...] = sum(low_ref[count + i].astype(F32) for i in range(3)) * 0.0625
    above_ref[...] = sum(high_ref[count + i].astype(F32) for i in range(3)) * 0.0625
    zero = jnp.zeros((ROWS, span), F32)
    sums = [[zero, zero] for _ in range(snaps)]
    for i in range(planes):
        p = (place_ref[2] + i) % planes
        metric_low = metric_ref[p, 0:ROWS, :] * 0.0625
        metric_high = metric_ref[p, rows - ROWS : rows, :] * 0.0625
        scale_low = jnp.where(row8 == 0, jnp.broadcast_to(below_ref[pl.ds(p, 1), :], (ROWS, span)), 0.0)
        scale_low = jnp.where(row8 == 1, pltpu.roll(metric_low, 1, 0), scale_low)
        scale_high = jnp.where(row8 == ROWS - 1, jnp.broadcast_to(above_ref[pl.ds(p, 1), :], (ROWS, span)), 0.0)
        scale_high = jnp.where(row8 == ROWS - 2, pltpu.roll(metric_high, ROWS - 1, 0), scale_high)
        for c in range(comps):
            low = low_ref[c * planes + p].astype(F32)
            high = high_ref[c * planes + p].astype(F32)
            for a in range(snaps):
                jump_low = u_ref[a, c, p, 0:ROWS, :].astype(F32) - pltpu.roll(low, (-2 * a) % ROWS, 0)
                jump_high = u_ref[a, c, p, rows - ROWS : rows, :].astype(F32) - pltpu.roll(
                    high, (ROWS - 2 - 2 * a) % ROWS, 0
                )
                edge_low = scale_low * jump_low
                edge_high = scale_high * jump_high
                sums[a][0] = sums[a][0] + edge_low * jump_low
                sums[a][1] = sums[a][1] + edge_high * jump_high
                out = jnp.concatenate(
                    [
                        part_ref[a, c, p, 0:ROWS, :] + edge_low,
                        part_ref[a, c, p, ROWS : rows - ROWS, :],
                        part_ref[a, c, p, rows - ROWS : rows, :] + edge_high,
                    ],
                    axis=0,
                ).astype(BF16)
                if i < half:
                    here_ref[a, c, i] = out
                else:
                    other_ref[a, c, i - half] = out
    for a in range(snaps):
        gain_ref[a, 0] = sums[a][0]
        gain_ref[a, 1] = sums[a][1]


def profile_kernel(planes, energy_ref, gain_ref, profile_ref):
    snaps, rows, span = energy_ref.shape
    row8 = sublane((ROWS, span))
    ones = jnp.ones((ROWS, span), F32)
    for a in range(snaps):
        first = jnp.where(row8 == 0, pltpu.roll(gain_ref[a, 0], ROWS - 1, 0), 0.0)
        last = jnp.where(row8 == ROWS - 1, pltpu.roll(gain_ref[a, 1], 1, 0), 0.0)
        energy = jnp.concatenate(
            [
                energy_ref[a, 0:ROWS, :] + first,
                energy_ref[a, ROWS : rows - ROWS, :],
                energy_ref[a, rows - ROWS : rows, :] + last,
            ],
            axis=0,
        )
        line = lax.dot_general(
            ones, energy, (((1,), (1,)), ((), ())), precision=lax.Precision.HIGHEST, preferred_element_type=F32
        )
        profile_ref[a : a + 1, :] = line[0:1, :] * (1.0 / (planes * span))


def pair_sums(sums, pairs, lefts, rights):
    lefts = [x.astype(F32) for x in lefts]
    rights = [x.astype(F32) for x in rights]
    out = list(sums)
    for t in range(0, lefts[0].shape[0], ROWS):
        for k, (a, b) in enumerate(pairs):
            out[k] = out[k] + lefts[a][t : t + ROWS] * rights[b][t : t + ROWS]
    return out


def totals(sums):
    tiles = []
    for start in range(0, len(sums), ROWS):
        tile = jnp.concatenate([jnp.sum(s, axis=0, keepdims=True) for s in sums[start : start + ROWS]], axis=0)
        tiles.append(jnp.broadcast_to(jnp.sum(tile, axis=1, keepdims=True), tile.shape))
    return tiles


def square_kernel(by_mate, place_ref, u_ref, here_ref, other_ref, block_ref):
    snaps, comps, planes, _, span = u_ref.shape
    half = planes // 2
    row, lane = sublane((ROWS, span)), lanes((ROWS, span))
    pairs = [(b, a) for b in range(snaps) for a in range(snaps) if by_mate or a <= b]
    sums = [jnp.zeros((ROWS, span), F32) for _ in pairs]
    for c in range(comps):
        for i in range(planes):
            p = (place_ref[2] + i) % planes
            ref = here_ref if i < half else other_ref
            sums = pair_sums(
                sums, pairs, [ref[b, c, i % half] for b in range(snaps)], [u_ref[a, c, p] for a in range(snaps)]
            )
    column = place_ref[1] if by_mate else place_ref[0]
    block = jnp.zeros((ROWS, span), F32)
    stacked = []
    for b in range(snaps):
        stacked += [sums[pairs.index((b, a) if (b, a) in pairs else (a, b))] for a in range(snaps)]
        stacked += [sums[0]] * (ROWS - snaps)
    for b, tile in enumerate(totals(stacked)):
        block = jnp.where((lane == column + b) & (row < snaps), tile, block)
    block_ref[...] = block


def cross_kernel(place_ref, got_ref, w_ref, forward_ref, back_ref):
    snaps, comps, planes, _, span = got_ref.shape
    group = ROWS // snaps
    lane, row = lanes((ROWS, span)), sublane((ROWS, span))
    pairs = [(i, j) for i in range(snaps) for j in range(snaps)]
    sums = [jnp.zeros((ROWS, span), F32) for _ in pairs]
    for c in range(comps):
        for i in range(planes):
            sums = pair_sums(
                sums, pairs, [w_ref[a, c, i] for a in range(snaps)], [got_ref[a, c, i] for a in range(snaps)]
            )
    order = [sums[i * snaps + j] for j in range(snaps) for i in range(snaps)]
    forward = jnp.zeros((ROWS, span), F32)
    for t, tile in enumerate(totals(order)):
        forward = forward + jnp.where(lane == place_ref[1] + t * group + row // snaps, tile, 0.0)
    back = jnp.zeros((ROWS, span), F32)
    for t, tile in enumerate(totals(sums)):
        back = back + jnp.where(lane == place_ref[0] + t * group + row // snaps, tile, 0.0)
    for ref, block in ((forward_ref, forward), (back_ref, back)):
        fold = block
        for i in range(1, group):
            fold = fold + pltpu.roll(block, i * snaps, 0)
        ref[...] = fold


def local(velocity, row_level, metric_table):
    snaps, comps, planes, rows, span = velocity.shape
    spaces, cores = lax.axis_size("space"), lax.axis_size("snap")
    chips = cores // 2
    z, s = lax.axis_index("space"), lax.axis_index("snap")
    chip, core = s // 2, s % 2
    mate = s + 1 - 2 * core
    half = planes // 2

    def begin(worker, other):
        return jnp.where(worker < other, 0, half)

    def ints(*values):
        return jnp.stack([jnp.asarray(x, jnp.int32) for x in values])

    def shape(*dims, dtype=BF16):
        return jax.ShapeDtypeStruct(dims, dtype)

    shifts = range(1, chips)
    starts = [begin(chip, (chip - k) % chips) for k in shifts]
    got = []
    for k in shifts:
        piece = lax.dynamic_slice_in_dim(velocity, begin((chip + k) % chips, chip), half, axis=2)
        got.append(lax.ppermute(piece, "snap", [(i, (i + 2 * k) % cores) for i in range(cores)]))

    row_ids = (z * rows + lax.iota(jnp.int32, rows)).astype(F32)
    stretch = 0.25 + 2.25 * row_ids / (rows * spaces - 1)
    chosen = row_level[:, None] == lax.iota(jnp.int32, metric_table.shape[1])[None, :]
    picked = jnp.sum(jnp.where(chosen[None], metric_table[:, None, :], 0.0), axis=2)
    metric = jnp.broadcast_to((picked / stretch)[:, :, None], (planes, rows, span))
    volume = jnp.broadcast_to((stretch / picked)[:, :, None], (planes, rows, span))
    packed = shape(comps * planes + 3, ROWS, span)
    up, down = call(pack_kernel, "pack", [packed, packed], [VMEM] * 2)(velocity, metric)

    def swap(array, first):
        pairs = []
        for i in range(spaces):
            j = ((i - first) ^ 1) + first
            alone = not 0 <= j < spaces
            pairs += [(i * cores + t, i * cores + (t ^ 1) if alone else j * cores + t) for t in range(cores)]
        return lax.ppermute(array, ("space", "snap"), pairs)

    odd = z % 2 == 1
    first = swap(jnp.where(odd, down, up), 0)
    second = swap(jnp.where(odd, up, down), 1)
    first, second, *got = lax.optimization_barrier((first, second, *got))
    low = jnp.where(z > 0, jnp.where(odd, first, second), 0)
    high = jnp.where(z < spaces - 1, jnp.where(odd, second, first), 0)

    operator = jnp.asarray(span_operator(span), BF16)
    part, energy = call(
        inner_kernel,
        "inner",
        [shape(*velocity.shape, dtype=F32), shape(snaps, rows, span, dtype=F32)],
        [VMEM] * 4,
        [pltpu.VMEM((planes, rows + 2 * ROWS, span), F32)] * 2,
    )(velocity, metric, volume, operator)
    own_at, mate_at = s * snaps, mate * snaps
    place = ints(own_at, mate_at, starts[0])
    halves = shape(snaps, comps, half, rows, span)
    here, other, gain = call(
        edge_kernel,
        "edges",
        [halves, halves, shape(snaps, 2, ROWS, span, dtype=F32)],
        [SMEM] + [VMEM] * 5,
        [pltpu.VMEM((ROWS, span), F32)] * 2,
    )(place, velocity, part, metric, low, high)

    def to_mate(array):
        return lax.ppermute(array, "snap", [(i, i ^ 1) for i in range(cores)])

    mate_here, mate_other = to_mate(here), to_mate(other)
    tile = shape(ROWS, span, dtype=F32)
    total = call(functools.partial(square_kernel, False), "square", tile, [SMEM] + [VMEM] * 3)(
        place, velocity, here, other
    )
    for_mate = 0
    back = []
    for k in shifts:
        source = 2 * ((chip - k) % chips) + core
        answer = []
        for at, set_here, set_other in ((own_at, here, other), (mate_at, mate_here, mate_other)):
            w = set_here if k == 1 else jnp.where(starts[k - 1] == starts[0], set_here, set_other)
            answer.append(
                call(cross_kernel, "cross", [tile, tile], [SMEM] + [VMEM] * 2)(
                    ints(at, source * snaps), got[k - 1], w
                )
            )
        total = total + answer[0][0]
        for_mate = for_mate + answer[1][0]
        back.append(answer[0][1] + answer[1][1])
    mates = call(functools.partial(square_kernel, True), "mates", tile, [SMEM] + [VMEM] * 3)(
        place, velocity, mate_here, mate_other
    )
    profile = call(
        functools.partial(profile_kernel, planes), "profile", shape(snaps, rows, dtype=F32), [VMEM] * 2
    )(energy, gain)
    for k in shifts:
        total = total + lax.ppermute(back[k - 1], "snap", [(i, (i - 2 * k) % cores) for i in range(cores)])
    total = total + to_mate(for_mate) + mates
    if spaces & (spaces - 1):
        gram = lax.psum(total, "space")
    else:
        gram = total
        step = 1
        while step < spaces:
            gram = gram + lax.ppermute(gram, "space", [(i, i ^ step) for i in range(spaces)])
            step *= 2
    gram = gram[:snaps, : snaps * cores] * (1.0 / (planes * rows * spaces * span))
    return gram, profile


def solution(mesh):
    in_specs = (P(("grp", "snap"), None, None, "space", None), P("space"), P())
    out_specs = (P(("grp", "snap"), None), P(("grp", "snap"), "space"))
    return jax.shard_map(local, mesh=mesh, in_specs=in_specs, out_specs=out_specs, check_vma=False)
```

```python
import functools

import jax
import jax.numpy as jnp
import numpy as np
from jax import lax
from jax.experimental import pallas as pl
from jax.experimental.pallas import tpu as pltpu
from jax.sharding import PartitionSpec as P

F32 = jnp.float32
BF16 = jnp.bfloat16
ROWS = 8
VMEM = pl.BlockSpec(memory_space=pltpu.VMEM)
OWN, MATE, FIRST, BASE, LAST, SEND = range(6)


def call(kernel, name, out_shape, scratch_shapes=()):
    single = not isinstance(out_shape, list)

    def run(*args):
        return pl.pallas_call(
            kernel,
            name=name,
            out_shape=out_shape,
            in_specs=[VMEM] * len(args),
            out_specs=VMEM if single else [VMEM] * len(out_shape),
            scratch_shapes=list(scratch_shapes),
            compiler_params=pltpu.CompilerParams(vmem_limit_bytes=16 * 2**20),
            cost_estimate=pl.CostEstimate(flops=0, bytes_accessed=0, transcendentals=0),
        )(*args)

    return run


def span_operator(cells):
    diff = np.zeros((cells, cells), np.float32)
    for i in range(cells):
        lo, hi = max(i - 1, 0), min(i + 1, cells - 1)
        scale = 0.5 / (hi - lo)
        diff[i, hi] += scale
        diff[i, lo] -= scale
    return diff.T @ diff


def sublane(shape):
    return lax.broadcasted_iota(jnp.int32, shape, len(shape) - 2)


def lanes(shape):
    return lax.broadcasted_iota(jnp.int32, shape, len(shape) - 1)


def tall(tile, rows):
    return jnp.concatenate([tile] * (rows // ROWS), axis=0)


def stretch_of(row_ids, last):
    return 0.25 + 2.25 * row_ids.astype(F32) / last.astype(F32)


def pack_kernel(place_ref, u_ref, up_ref, down_ref, *pieces):
    snaps, comps, planes, rows, span = u_ref.shape
    half = planes // 2
    row8 = sublane((ROWS, span))
    for k, piece in enumerate(pieces):
        to_first = tall(place_ref[SEND + k], rows) > 0
        for a in range(snaps):
            for c in range(comps):
                for i in range(half):
                    both = u_ref[a, c, i].astype(F32), u_ref[a, c, i + half].astype(F32)
                    piece[a, c, i] = jnp.where(to_first, *both).astype(BF16)
    for c in range(comps):
        for p in range(planes):
            up = jnp.zeros((ROWS, span), F32)
            down = jnp.zeros((ROWS, span), F32)
            for a in range(snaps):
                mine = row8 // 2 == a
                first = u_ref[a, c, p, 0:ROWS, :].astype(F32)
                last = u_ref[a, c, p, rows - ROWS : rows, :].astype(F32)
                up = jnp.where(mine, pltpu.roll(last, (2 * a + 2) % ROWS, 0), up)
                down = jnp.where(mine, pltpu.roll(first, (2 * a) % ROWS, 0), down)
            up_ref[c * planes + p] = up.astype(BF16)
            down_ref[c * planes + p] = down.astype(BF16)


def metric_kernel(place_ref, level_ref, table_ref, metric_ref, volume_ref):
    planes, rows, span = metric_ref.shape
    levels = table_ref.shape[1]
    level = jnp.broadcast_to(level_ref[0:1, 0:rows], (rows, rows))
    level = jnp.where(sublane((rows, rows)) == lanes((rows, rows)), level, 0).astype(F32)
    level = jnp.sum(level, axis=1, keepdims=True).astype(jnp.int32)
    chosen = jnp.broadcast_to(level, (rows, levels)) == lanes((rows, levels))
    stretch = stretch_of(tall(place_ref[BASE], rows) + sublane((rows, span)), tall(place_ref[LAST], rows))
    for p in range(planes):
        picked = jnp.sum(jnp.where(chosen, table_ref[p : p + 1, :], 0.0), axis=1, keepdims=True)
        picked = jnp.broadcast_to(picked, (rows, span))
        metric_ref[p] = picked / stretch
        volume_ref[p] = stretch / picked


def entry_kernel(rows, level_ref, entry_ref):
    row8, lane = sublane(level_ref.shape), lanes(level_ref.shape)
    for i, j in enumerate((rows - 1, 0)):
        level = jnp.sum(jnp.where(lane == j, level_ref[...], 0).astype(F32), axis=1, keepdims=True)
        level = jnp.broadcast_to(level, level_ref.shape)
        high = jnp.floor(level * (1.0 / 128.0))
        entry = jnp.where(row8 == 0, high, jnp.where(row8 == 1, level - 128.0 * high, 1.0))
        entry_ref[i, 0] = entry.astype(BF16)


def inner_kernel(u_ref, mate_ref, metric_ref, volume_ref, op_ref, part_ref, mate_part_ref, energy_ref, f_ref, e_ref):
    snaps, comps, planes, rows, span = u_ref.shape
    first, end = ROWS, ROWS + rows
    row = sublane((rows, span))
    within = (row > 0) & (row < rows - 1)
    for a in range(snaps):
        energy_ref[a] = jnp.zeros((rows, span), F32)
    for p in range(planes):
        f_ref[p, 0:first, :] = jnp.zeros((ROWS, span), F32)
        f_ref[p, end : end + ROWS, :] = jnp.zeros((ROWS, span), F32)
        e_ref[p, 0:first, :] = jnp.zeros((ROWS, span), F32)
        e_ref[p, end : end + ROWS, :] = jnp.zeros((ROWS, span), F32)

    def operate(source, target, a, c, energy):
        raw = source[a, c]
        spanned = jnp.dot(raw.reshape(planes * rows, span), op_ref[...], preferred_element_type=F32)
        spanned = spanned.reshape(planes, rows, span)
        u = raw.astype(F32)
        for p in range(planes):
            f_ref[p, first:end, :] = u[p]
        stream = [None] * planes
        for i in range(planes):
            lo, hi = max(i - 1, 0), min(i + 1, planes - 1)
            scale = 0.25 / (hi - lo) ** 2
            edge = (volume_ref[i] * scale) * (u[hi] - u[lo])
            stream[hi] = edge if stream[hi] is None else stream[hi] + edge
            stream[lo] = -edge if stream[lo] is None else stream[lo] - edge
        total = energy[a] if energy is not None else None
        for p in range(planes):
            jump = f_ref[p, first + 1 : end + 1, :] - f_ref[p, first - 1 : end - 1, :]
            edge = jnp.where(within, (metric_ref[p] * 0.0625) * jump, 0.0)
            e_ref[p, first:end, :] = edge
            partial = volume_ref[p] * (u[p] + spanned[p]) + stream[p]
            if energy is not None:
                total = total + (u[p] * partial + edge * jump)
            normal = e_ref[p, first - 1 : end - 1, :] - e_ref[p, first + 1 : end + 1, :]
            target[a, c, p] = partial + normal
        if energy is not None:
            energy[a] = total

    def field(c, carry):
        for a in range(snaps):
            operate(u_ref, part_ref, a, c, energy_ref)
        return carry

    def mate_field(c, carry):
        for a in range(snaps):
            operate(mate_ref, mate_part_ref, a, c, None)
        return carry

    lax.fori_loop(0, comps, field, 0)
    lax.fori_loop(0, comps, mate_field, 0)


def edge_kernel(
    place_ref, table_ref, u_ref, mate_ref, part_ref, mate_part_ref, metric_ref, low_ref, high_ref, gain_ref, *refs
):
    snaps, comps, planes, rows, span = u_ref.shape
    count = comps * planes
    levels = table_ref.shape[1]
    half = planes // 2
    row8 = sublane((ROWS, span))
    is_first = tall(place_ref[FIRST], rows) > 0
    factors = []
    for ref, offset in ((low_ref, -1), (high_ref, rows)):
        sent = ref[2 * count].astype(F32)
        level = (128.0 * sent[0:1, :] + sent[1:2, :]).astype(jnp.int32)
        chosen = lanes((planes, levels)) == jnp.broadcast_to(level[:, 0:1], (planes, levels))
        picked = jnp.sum(jnp.where(chosen, table_ref[...], 0.0), axis=1, keepdims=True)
        stretch = stretch_of(place_ref[BASE][0:1, :] + offset, place_ref[LAST][0:1, :])
        exists = sent[2:3, :] > 0.0
        factors.append(jnp.where(exists, jnp.broadcast_to(picked, (planes, span)) / stretch * 0.0625, 0.0))
    below, above = factors
    scales = []
    for p in range(planes):
        metric_low = metric_ref[p, 0:ROWS, :] * 0.0625
        metric_high = metric_ref[p, rows - ROWS : rows, :] * 0.0625
        scale_low = jnp.where(row8 == 0, jnp.broadcast_to(below[p : p + 1, :], (ROWS, span)), 0.0)
        scale_low = jnp.where(row8 == 1, pltpu.roll(metric_low, 1, 0), scale_low)
        scale_high = jnp.where(row8 == ROWS - 1, jnp.broadcast_to(above[p : p + 1, :], (ROWS, span)), 0.0)
        scale_high = jnp.where(row8 == ROWS - 2, pltpu.roll(metric_high, ROWS - 1, 0), scale_high)
        scales.append((scale_low, scale_high))
    zero = jnp.zeros((ROWS, span), F32)
    sums = [[zero, zero] for _ in range(snaps)]
    work = [(u_ref, part_ref, 0, refs[0], refs[1]), (mate_ref, mate_part_ref, count, refs[2], (refs[3:] or [None])[0])]
    for source, part, offset, here, other in work:
        for i in range(half):
            for c in range(comps):
                at = offset + c * planes + i
                halos = [(low_ref[p].astype(F32), high_ref[p].astype(F32)) for p in (at, at + half)]
                for a in range(snaps):
                    outs = []
                    for p, (low, high) in zip((i, i + half), halos):
                        jump_low = source[a, c, p, 0:ROWS, :].astype(F32) - pltpu.roll(low, (-2 * a) % ROWS, 0)
                        jump_high = source[a, c, p, rows - ROWS : rows, :].astype(F32) - pltpu.roll(
                            high, (ROWS - 2 - 2 * a) % ROWS, 0
                        )
                        edge_low = scales[p][0] * jump_low
                        edge_high = scales[p][1] * jump_high
                        if source is u_ref:
                            sums[a][0] = sums[a][0] + edge_low * jump_low
                            sums[a][1] = sums[a][1] + edge_high * jump_high
                        outs.append(
                            jnp.concatenate(
                                [
                                    part[a, c, p, 0:ROWS, :] + edge_low,
                                    part[a, c, p, ROWS : rows - ROWS, :],
                                    part[a, c, p, rows - ROWS : rows, :] + edge_high,
                                ],
                                axis=0,
                            )
                        )
                    here[a, c, i] = jnp.where(is_first, outs[0], outs[1]).astype(BF16)
                    if other is not None:
                        other[a, c, i] = jnp.where(is_first, outs[1], outs[0]).astype(BF16)
    for a in range(snaps):
        gain_ref[a, 0] = sums[a][0]
        gain_ref[a, 1] = sums[a][1]


def profile_kernel(planes, energy_ref, gain_ref, profile_ref):
    snaps, rows, span = energy_ref.shape
    row8 = sublane((ROWS, span))
    ones = jnp.ones((ROWS, span), F32)
    for a in range(snaps):
        first = jnp.where(row8 == 0, pltpu.roll(gain_ref[a, 0], ROWS - 1, 0), 0.0)
        last = jnp.where(row8 == ROWS - 1, pltpu.roll(gain_ref[a, 1], 1, 0), 0.0)
        energy = jnp.concatenate(
            [
                energy_ref[a, 0:ROWS, :] + first,
                energy_ref[a, ROWS : rows - ROWS, :],
                energy_ref[a, rows - ROWS : rows, :] + last,
            ],
            axis=0,
        )
        line = lax.dot_general(
            ones, energy, (((1,), (1,)), ((), ())), precision=lax.Precision.HIGHEST, preferred_element_type=F32
        )
        profile_ref[a : a + 1, :] = line[0:1, :] * (1.0 / (planes * span))


def pair_sums(sums, pairs, lefts, rights):
    lefts = [x.astype(F32) for x in lefts]
    rights = [x.astype(F32) for x in rights]
    out = list(sums)
    for t in range(0, lefts[0].shape[0], ROWS):
        for k, (a, b) in enumerate(pairs):
            out[k] = out[k] + lefts[a][t : t + ROWS] * rights[b][t : t + ROWS]
    return out


def totals(sums):
    tiles = []
    for start in range(0, len(sums), ROWS):
        tile = jnp.concatenate([jnp.sum(s, axis=0, keepdims=True) for s in sums[start : start + ROWS]], axis=0)
        tiles.append(jnp.broadcast_to(jnp.sum(tile, axis=1, keepdims=True), tile.shape))
    return tiles


def square_kernel(by_mate, place_ref, u_ref, here_ref, other_ref, block_ref):
    snaps, comps, planes, rows, span = u_ref.shape
    half = planes // 2
    row, lane = sublane((ROWS, span)), lanes((ROWS, span))
    is_first = tall(place_ref[FIRST], rows) > 0
    pairs = [(b, a) for b in range(snaps) for a in range(snaps) if by_mate or a <= b]
    sums = [jnp.zeros((ROWS, span), F32) for _ in pairs]
    for c in range(comps):
        for i in range(half):
            both = [(u_ref[a, c, i].astype(F32), u_ref[a, c, i + half].astype(F32)) for a in range(snaps)]
            u_here = [jnp.where(is_first, x, y) for x, y in both]
            u_other = [jnp.where(is_first, y, x) for x, y in both]
            sums = pair_sums(sums, pairs, u_here, [here_ref[b, c, i] for b in range(snaps)])
            sums = pair_sums(sums, pairs, u_other, [other_ref[b, c, i] for b in range(snaps)])
    column = place_ref[MATE] if by_mate else place_ref[OWN]
    block = jnp.zeros((ROWS, span), F32)
    stacked = []
    for b in range(snaps):
        stacked += [sums[pairs.index((b, a) if (b, a) in pairs else (a, b))] for a in range(snaps)]
        stacked += [sums[0]] * (ROWS - snaps)
    for b, tile in enumerate(totals(stacked)):
        block = jnp.where((lane == column + b) & (row < snaps), tile, block)
    block_ref[...] = block


def cross_kernel(place_ref, source_ref, got_ref, w_ref, mate_ref, own_ref, for_mate_ref, back_ref):
    snaps, comps, half, _, span = got_ref.shape
    group = ROWS // snaps
    lane, row = lanes((ROWS, span)), sublane((ROWS, span))
    pairs = [(i, j) for i in range(2 * snaps) for j in range(snaps)]
    sums = [jnp.zeros((ROWS, span), F32) for _ in pairs]
    for c in range(comps):
        for i in range(half):
            left = [ref[a, c, i] for ref in (w_ref, mate_ref) for a in range(snaps)]
            sums = pair_sums(sums, pairs, left, [got_ref[a, c, i] for a in range(snaps)])
    ahead = jnp.zeros((ROWS, span), F32)
    flipped = [sums[i * snaps + j] for j in range(snaps) for i in range(2 * snaps)]
    for t, tile in enumerate(totals(flipped)):
        ahead = ahead + jnp.where(lane == source_ref[...] + t, tile, 0.0)
    own_ref[...] = jnp.where(row < snaps, ahead, 0.0)
    for_mate_ref[...] = jnp.where(row < snaps, pltpu.roll(ahead, ROWS - snaps, 0), 0.0)
    back = jnp.zeros((ROWS, span), F32)
    for t, tile in enumerate(totals(sums)):
        i = t * group + row // snaps
        column = jnp.where(i < snaps, place_ref[OWN] + i, place_ref[MATE] + i - snaps)
        back = back + jnp.where(lane == column, tile, 0.0)
    fold = back
    for i in range(1, group):
        fold = fold + pltpu.roll(back, i * snaps, 0)
    back_ref[...] = fold


def local(velocity, row_level, metric_table):
    snaps, comps, planes, rows, span = velocity.shape
    spaces, cores = lax.axis_size("space"), lax.axis_size("snap")
    chips = cores // 2
    z, s = lax.axis_index("space"), lax.axis_index("snap")
    chip, core = s // 2, s % 2
    mate = s + 1 - 2 * core
    half = planes // 2
    shifts = range(1, chips)

    def shape(*dims, dtype=BF16):
        return jax.ShapeDtypeStruct(dims, dtype)

    def tiles(*values):
        values = jnp.stack([jnp.asarray(x, jnp.int32) for x in values])
        return jnp.broadcast_to(values[:, None, None], (values.shape[0], ROWS, span))

    def to_mate(array):
        return lax.ppermute(array, "snap", [(i, i ^ 1) for i in range(cores)])

    def begins(worker, other):
        return worker < other

    starts = [begins(chip, (chip - k) % chips) for k in shifts]
    place = tiles(
        s * snaps,
        mate * snaps,
        starts[0],
        z * rows,
        rows * spaces - 1,
        *[begins((chip + k) % chips, chip) for k in shifts],
    )
    packed = shape(comps * planes, ROWS, span)
    piece = shape(snaps, comps, half, rows, span)
    up, down, *pieces = call(pack_kernel, "pack", [packed, packed] + [piece] * (chips - 1))(place, velocity)
    got = [
        lax.ppermute(piece, "snap", [(i, (i + 2 * k) % cores) for i in range(cores)])
        for k, piece in zip(shifts, pieces)
    ]
    u_mate = to_mate(velocity)

    odd = z % 2 == 1
    edge_rows = jnp.stack([up, down])
    edge_rows = jnp.concatenate([edge_rows, to_mate(edge_rows)], axis=1)
    levels = jnp.broadcast_to(jnp.pad(row_level, (0, span - rows)), (ROWS, span))
    entry = call(functools.partial(entry_kernel, rows), "entry", shape(2, 1, ROWS, span))(levels)
    sent = jnp.concatenate([edge_rows, entry], axis=1)

    def swap(array, first):
        pairs = []
        for i in range(spaces):
            j = ((i - first) ^ 1) + first
            alone = not 0 <= j < spaces
            pairs += [(i * cores + t, i * cores + (t ^ 1) if alone else j * cores + t) for t in range(cores)]
        return lax.ppermute(array, ("space", "snap"), pairs)

    first = swap(jnp.where(odd, sent[1], sent[0]), 0)
    second = swap(jnp.where(odd, sent[0], sent[1]), 1)
    factor = shape(planes, rows, span, dtype=F32)
    metric, volume = call(metric_kernel, "metric", [factor, factor])(place, levels, metric_table)
    operator = jnp.asarray(span_operator(span), BF16)
    scratch = [pltpu.VMEM((planes, rows + 2 * ROWS, span), F32)] * 2
    full = shape(*velocity.shape, dtype=F32)
    part, part_mate, energy = call(inner_kernel, "inner", [full, full, shape(snaps, rows, span, dtype=F32)], scratch)(
        velocity, u_mate, metric, volume, operator
    )
    first, second, part, *got = lax.optimization_barrier((first, second, part, *got))
    low = jnp.where(z > 0, jnp.where(odd, first, second), 0)
    high = jnp.where(z < spaces - 1, jnp.where(odd, second, first), 0)

    gain, here, other, *mates = call(
        edge_kernel, "edges", [shape(snaps, 2, ROWS, span, dtype=F32)] + [piece] * (2 + min(2, chips - 1))
    )(place, metric_table, velocity, u_mate, part, part_mate, metric, low, high)

    tile = shape(ROWS, span, dtype=F32)
    total, for_mate, back = 0, 0, []
    for k in shifts:
        source = tiles((2 * ((chip - k) % chips) + core) * snaps)[0]
        w, w_mate = here, mates[0]
        if k > 1:
            same = starts[k - 1] == starts[0]
            w, w_mate = jnp.where(same, here, other), jnp.where(same, mates[0], mates[1])
        answer = call(cross_kernel, "cross", [tile] * 3)(place, source, got[k - 1], w, w_mate)
        total = total + answer[0]
        for_mate = for_mate + answer[1]
        back.append(answer[2])
    total = total + call(functools.partial(square_kernel, False), "square", tile)(place, velocity, here, other)
    total = total + call(functools.partial(square_kernel, True), "mates", tile)(place, u_mate, here, other)
    profile = call(functools.partial(profile_kernel, planes), "profile", shape(snaps, rows, dtype=F32))(energy, gain)
    for k in shifts:
        total = total + lax.ppermute(back[k - 1], "snap", [(i, (i - 2 * k) % cores) for i in range(cores)])
    total = total + to_mate(for_mate)
    if spaces & (spaces - 1):
        gram = lax.psum(total, "space")
    else:
        gram = total
        step = 1
        while step < spaces:
            gram = gram + lax.ppermute(gram, "space", [(i, i ^ step) for i in range(spaces)])
            step *= 2
    gram = gram[:snaps, : snaps * cores] * (1.0 / (planes * rows * spaces * span))
    return gram, profile


def solution(mesh):
    in_specs = (P(("grp", "snap"), None, None, "space", None), P("space"), P())
    out_specs = (P(("grp", "snap"), None), P(("grp", "snap"), "space"))
    return jax.shard_map(local, mesh=mesh, in_specs=in_specs, out_specs=out_specs, check_vma=False)
```

```python
import functools

import jax
import jax.numpy as jnp
import numpy as np
from jax import lax
from jax.experimental import pallas as pl
from jax.experimental.pallas import tpu as pltpu
from jax.sharding import PartitionSpec as P

F32 = jnp.float32
BF16 = jnp.bfloat16
ROWS = 8
VMEM = pl.BlockSpec(memory_space=pltpu.VMEM)


def call(kernel, name, out_shape, scratch_shapes=()):
    single = not isinstance(out_shape, list)

    def run(*args):
        return pl.pallas_call(
            kernel,
            name=name,
            out_shape=out_shape,
            in_specs=[VMEM] * len(args),
            out_specs=VMEM if single else [VMEM] * len(out_shape),
            scratch_shapes=list(scratch_shapes),
            compiler_params=pltpu.CompilerParams(vmem_limit_bytes=16 * 2**20),
            cost_estimate=pl.CostEstimate(flops=0, bytes_accessed=0, transcendentals=0),
        )(*args)

    return run


def span_operator(cells):
    diff = np.zeros((cells, cells), np.float32)
    for i in range(cells):
        lo, hi = max(i - 1, 0), min(i + 1, cells - 1)
        scale = 0.5 / (hi - lo)
        diff[i, hi] += scale
        diff[i, lo] -= scale
    return diff.T @ diff


def sublane(shape):
    return lax.broadcasted_iota(jnp.int32, shape, len(shape) - 2)


def lanes(shape):
    return lax.broadcasted_iota(jnp.int32, shape, len(shape) - 1)


def stretch_of(row_ids, rows):
    z, spaces = lax.axis_index("space"), lax.axis_size("space")
    return 0.25 + 2.25 * (row_ids + z * rows).astype(F32) / (rows * spaces - 1)


def half_here(k, planes):
    chips = lax.axis_size("snap") // 2
    chip = lax.axis_index("snap") // 2
    return jnp.where(chip < (chip + chips - k) % chips, 0, planes // 2)


def piece_kernel(u_ref, *pieces):
    snaps, comps, planes, _, _ = u_ref.shape
    half = planes // 2
    chips = len(pieces) + 1
    chip = lax.axis_index("snap") // 2
    for k, piece in enumerate(pieces):
        start = jnp.where((chip + k + 1) % chips < chip, 0, half)
        for a in range(snaps):
            for c in range(comps):
                for i in range(half):
                    piece[a, c, i] = u_ref[a, c, start + i]


def pack_kernel(mate_planes, level_ref, u_ref, mate_ref, first_ref, second_ref):
    snaps, comps, planes, rows, span = u_ref.shape
    count = comps * planes
    row8, lane = sublane((ROWS, span)), lanes((ROWS, span))
    odd = lax.axis_index("space") % 2 == 1

    def put(at, up, down):
        first_ref[at] = jnp.where(odd, down, up).astype(BF16)
        second_ref[at] = jnp.where(odd, up, down).astype(BF16)

    entries = []
    for j in (rows - 1, 0):
        level = jnp.sum(jnp.where(lane == j, level_ref[...], 0).astype(F32), axis=1, keepdims=True)
        level = jnp.broadcast_to(level, (ROWS, span))
        high = jnp.floor(level * (1.0 / 128.0))
        entries.append(jnp.where(row8 == 0, high, jnp.where(row8 == 1, level - 128.0 * high, 1.0)))
    put(first_ref.shape[0] - 1, *entries)
    for offset, ref, size in ((0, u_ref, planes), (count, mate_ref, mate_planes)):
        for c in range(comps):
            for i in range(size):
                p = i if size == planes else half_here(1, planes) + i
                up = jnp.zeros((ROWS, span), F32)
                down = jnp.zeros((ROWS, span), F32)
                for a in range(snaps):
                    mine = row8 // 2 == a
                    first = ref[a, c, p, 0:ROWS, :].astype(F32)
                    last = ref[a, c, p, rows - ROWS : rows, :].astype(F32)
                    up = jnp.where(mine, pltpu.roll(last, (2 * a + 2) % ROWS, 0), up)
                    down = jnp.where(mine, pltpu.roll(first, (2 * a) % ROWS, 0), down)
                put(offset + c * size + i, up, down)


def metric_kernel(level_ref, table_ref, metric_ref, volume_ref):
    planes, rows, span = metric_ref.shape
    levels = table_ref.shape[1]
    level = jnp.broadcast_to(level_ref[0:1, 0:rows], (rows, rows))
    level = jnp.where(sublane((rows, rows)) == lanes((rows, rows)), level, 0).astype(F32)
    level = jnp.sum(level, axis=1, keepdims=True).astype(jnp.int32)
    chosen = jnp.broadcast_to(level, (rows, levels)) == lanes((rows, levels))
    stretch = stretch_of(sublane((rows, span)), rows)
    for p in range(planes):
        picked = jnp.sum(jnp.where(chosen, table_ref[p : p + 1, :], 0.0), axis=1, keepdims=True)
        picked = jnp.broadcast_to(picked, (rows, span))
        metric_ref[p] = picked / stretch
        volume_ref[p] = stretch / picked


def inner_kernel(u_ref, mate_ref, metric_ref, volume_ref, op_ref, part_ref, mate_part_ref, energy_ref, f_ref, e_ref):
    snaps, comps, planes, rows, span = u_ref.shape
    first, end = ROWS, ROWS + rows
    row = sublane((rows, span))
    within = (row > 0) & (row < rows - 1)
    for a in range(snaps):
        energy_ref[a] = jnp.zeros((rows, span), F32)
    for p in range(planes):
        f_ref[p, 0:first, :] = jnp.zeros((ROWS, span), F32)
        f_ref[p, end : end + ROWS, :] = jnp.zeros((ROWS, span), F32)
        e_ref[p, 0:first, :] = jnp.zeros((ROWS, span), F32)
        e_ref[p, end : end + ROWS, :] = jnp.zeros((ROWS, span), F32)

    def operate(source, target, a, c, energy):
        raw = source[a, c]
        spanned = jnp.dot(raw.reshape(planes * rows, span), op_ref[...], preferred_element_type=F32)
        spanned = spanned.reshape(planes, rows, span)
        u = raw.astype(F32)
        for p in range(planes):
            f_ref[p, first:end, :] = u[p]
        stream = [None] * planes
        for i in range(planes):
            lo, hi = max(i - 1, 0), min(i + 1, planes - 1)
            scale = 0.25 / (hi - lo) ** 2
            edge = (volume_ref[i] * scale) * (u[hi] - u[lo])
            stream[hi] = edge if stream[hi] is None else stream[hi] + edge
            stream[lo] = -edge if stream[lo] is None else stream[lo] - edge
        total = energy[a] if energy is not None else None
        for p in range(planes):
            jump = f_ref[p, first + 1 : end + 1, :] - f_ref[p, first - 1 : end - 1, :]
            edge = jnp.where(within, (metric_ref[p] * 0.0625) * jump, 0.0)
            e_ref[p, first:end, :] = edge
            partial = volume_ref[p] * (u[p] + spanned[p]) + stream[p]
            if energy is not None:
                total = total + (u[p] * partial + edge * jump)
            normal = e_ref[p, first - 1 : end - 1, :] - e_ref[p, first + 1 : end + 1, :]
            target[a, c, p] = partial + normal
        if energy is not None:
            energy[a] = total

    def field(c, carry):
        for a in range(snaps):
            operate(u_ref, part_ref, a, c, energy_ref)
        return carry

    def mate_field(c, carry):
        for a in range(snaps):
            operate(mate_ref, mate_part_ref, a, c, None)
        return carry

    lax.fori_loop(0, comps, field, 0)
    lax.fori_loop(0, comps, mate_field, 0)


def edge_scales(table_ref, metric_ref, low_ref, high_ref):
    planes, rows, span = metric_ref.shape
    levels = table_ref.shape[1]
    row8 = sublane((ROWS, span))
    factors = []
    for ref, offset in ((low_ref, -1), (high_ref, rows)):
        sent = ref[ref.shape[0] - 1].astype(F32)
        level = (128.0 * sent[0:1, :] + sent[1:2, :]).astype(jnp.int32)
        chosen = lanes((planes, levels)) == jnp.broadcast_to(level[:, 0:1], (planes, levels))
        picked = jnp.sum(jnp.where(chosen, table_ref[...], 0.0), axis=1, keepdims=True)
        stretch = stretch_of(jnp.full((1, span), offset, jnp.int32), rows)
        exists = sent[2:3, :] > 0.0
        factors.append(jnp.where(exists, jnp.broadcast_to(picked, (planes, span)) / stretch * 0.0625, 0.0))
    below, above = factors
    scales = []
    for p in range(planes):
        metric_low = metric_ref[p, 0:ROWS, :] * 0.0625
        metric_high = metric_ref[p, rows - ROWS : rows, :] * 0.0625
        scale_low = jnp.where(row8 == 0, jnp.broadcast_to(below[p : p + 1, :], (ROWS, span)), 0.0)
        scale_low = jnp.where(row8 == 1, pltpu.roll(metric_low, 1, 0), scale_low)
        scale_high = jnp.where(row8 == ROWS - 1, jnp.broadcast_to(above[p : p + 1, :], (ROWS, span)), 0.0)
        scale_high = jnp.where(row8 == ROWS - 2, pltpu.roll(metric_high, ROWS - 1, 0), scale_high)
        scales.append((scale_low, scale_high))
    return scales


def edges_at(scale, u, low, high, a):
    jump_low = u[0:ROWS] - pltpu.roll(low, (-2 * a) % ROWS, 0)
    jump_high = u[-ROWS:] - pltpu.roll(high, (ROWS - 2 - 2 * a) % ROWS, 0)
    edge_low, edge_high = scale[0] * jump_low, scale[1] * jump_high
    return edge_low, edge_high, edge_low * jump_low, edge_high * jump_high


def edge_kernel(table_ref, u_ref, part_ref, metric_ref, low_ref, high_ref, w_ref, gain_ref):
    snaps, comps, planes, rows, span = u_ref.shape
    scales = edge_scales(table_ref, metric_ref, low_ref, high_ref)
    zero = jnp.zeros((ROWS, span), F32)
    sums = [[zero, zero] for _ in range(snaps)]
    for c in range(comps):
        for p in range(planes):
            low, high = low_ref[c * planes + p].astype(F32), high_ref[c * planes + p].astype(F32)
            for a in range(snaps):
                edges = edges_at(scales[p], u_ref[a, c, p].astype(F32), low, high, a)
                sums[a] = [x + y for x, y in zip(sums[a], edges[2:])]
                part = part_ref[a, c, p]
                w_ref[a, c, p] = jnp.concatenate(
                    [part[0:ROWS] + edges[0], part[ROWS : rows - ROWS], part[rows - ROWS :] + edges[1]], axis=0
                ).astype(BF16)
    for a in range(snaps):
        gain_ref[a, 0] = sums[a][0]
        gain_ref[a, 1] = sums[a][1]


def profile_kernel(planes, energy_ref, gain_ref, profile_ref):
    snaps, rows, span = energy_ref.shape
    row8 = sublane((ROWS, span))
    ones = jnp.ones((ROWS, span), F32)
    for a in range(snaps):
        first = jnp.where(row8 == 0, pltpu.roll(gain_ref[a, 0], ROWS - 1, 0), 0.0)
        last = jnp.where(row8 == ROWS - 1, pltpu.roll(gain_ref[a, 1], 1, 0), 0.0)
        energy = jnp.concatenate(
            [
                energy_ref[a, 0:ROWS, :] + first,
                energy_ref[a, ROWS : rows - ROWS, :],
                energy_ref[a, rows - ROWS : rows, :] + last,
            ],
            axis=0,
        )
        line = lax.dot_general(
            ones, energy, (((1,), (1,)), ((), ())), precision=lax.Precision.HIGHEST, preferred_element_type=F32
        )
        profile_ref[a : a + 1, :] = line[0:1, :] * (1.0 / (planes * span))


def pair_sums(sums, pairs, lefts, rights):
    lefts = [x.astype(F32) for x in lefts]
    rights = [x.astype(F32) for x in rights]
    out = list(sums)
    for t in range(0, lefts[0].shape[0], ROWS):
        for k, (a, b) in enumerate(pairs):
            out[k] = out[k] + lefts[a][t : t + ROWS] * rights[b][t : t + ROWS]
    return out


def totals(sums):
    tiles = []
    for start in range(0, len(sums), ROWS):
        tile = jnp.concatenate([jnp.sum(s, axis=0, keepdims=True) for s in sums[start : start + ROWS]], axis=0)
        tiles.append(jnp.broadcast_to(jnp.sum(tile, axis=1, keepdims=True), tile.shape))
    return tiles


def square_kernel(by_mate, u_ref, w_ref, block_ref):
    snaps, comps, planes, rows, span = u_ref.shape
    row, lane = sublane((ROWS, span)), lanes((ROWS, span))
    pairs = [(b, a) for b in range(snaps) for a in range(snaps) if by_mate or a <= b]
    sums = [jnp.zeros((ROWS, span), F32) for _ in pairs]
    for c in range(comps):
        for p in range(planes):
            sums = pair_sums(
                sums, pairs, [u_ref[b, c, p] for b in range(snaps)], [w_ref[a, c, p] for a in range(snaps)]
            )
    core = lax.axis_index("snap")
    column = snaps * (core + 1 - 2 * (core % 2) if by_mate else core)
    block = jnp.zeros((ROWS, span), F32)
    stacked = []
    for b in range(snaps):
        stacked += [sums[pairs.index((b, a) if (b, a) in pairs else (a, b))] for a in range(snaps)]
        stacked += [sums[0]] * (ROWS - snaps)
    for b, tile in enumerate(totals(stacked)):
        block = jnp.where((lane == column + b) & (row < snaps), tile, block)
    block_ref[...] = block


def cross_kernel(
    k, table_ref, u_ref, mate_ref, part_ref, mate_part_ref, metric_ref, low_ref, high_ref, got_ref,
    own_ref, for_mate_ref, back_ref, scale_ref,
):
    snaps, comps, half, rows, span = got_ref.shape
    planes = 2 * half
    count = comps * planes
    group = ROWS // snaps
    mate_planes = (low_ref.shape[0] - 1 - count) // comps
    start = half_here(k, planes)
    for p, (low, high) in enumerate(edge_scales(table_ref, metric_ref, low_ref, high_ref)):
        scale_ref[p, 0] = low
        scale_ref[p, 1] = high
    lane, row = lanes((ROWS, span)), sublane((ROWS, span))
    pairs = [(i, j) for i in range(2 * snaps) for j in range(snaps)]
    sums = [jnp.zeros((ROWS, span), F32) for _ in pairs]
    for c in range(comps):
        for i in range(half):
            p = start + i
            scale = scale_ref[p, 0], scale_ref[p, 1]
            at_mate = count + c * mate_planes + (p if mate_planes == planes else i)
            left = []
            for u, part, at in ((u_ref, part_ref, c * planes + p), (mate_ref, mate_part_ref, at_mate)):
                low, high = low_ref[at].astype(F32), high_ref[at].astype(F32)
                for a in range(snaps):
                    edges = edges_at(scale, u[a, c, p].astype(F32), low, high, a)
                    w = part[a, c, p]
                    left.append(
                        jnp.concatenate(
                            [w[0:ROWS] + edges[0], w[ROWS : rows - ROWS], w[rows - ROWS :] + edges[1]], axis=0
                        )
                    )
            sums = pair_sums(sums, pairs, left, [got_ref[a, c, i] for a in range(snaps)])
    cores = lax.axis_size("snap")
    core = lax.axis_index("snap")
    own, mate = core * snaps, (core + 1 - 2 * (core % 2)) * snaps
    source = (core + cores - 2 * k) % cores * snaps
    ahead = jnp.zeros((ROWS, span), F32)
    flipped = [sums[i * snaps + j] for j in range(snaps) for i in range(2 * snaps)]
    for t, tile in enumerate(totals(flipped)):
        ahead = ahead + jnp.where(lane == source + t, tile, 0.0)
    own_ref[...] = jnp.where(row < snaps, ahead, 0.0)
    for_mate_ref[...] = jnp.where(row < snaps, pltpu.roll(ahead, ROWS - snaps, 0), 0.0)
    back = jnp.zeros((ROWS, span), F32)
    for t, tile in enumerate(totals(sums)):
        i = t * group + row // snaps
        back = back + jnp.where(lane == jnp.where(i < snaps, own + i, mate + i - snaps), tile, 0.0)
    fold = back
    for i in range(1, group):
        fold = fold + pltpu.roll(back, i * snaps, 0)
    back_ref[...] = fold


def local(velocity, row_level, metric_table):
    snaps, comps, planes, rows, span = velocity.shape
    spaces, cores = lax.axis_size("space"), lax.axis_size("snap")
    chips = cores // 2
    z = lax.axis_index("space")
    half = planes // 2
    shifts = range(1, chips)

    def shape(*dims, dtype=BF16):
        return jax.ShapeDtypeStruct(dims, dtype)

    def to_mate(array):
        return lax.ppermute(array, "snap", [(i, i ^ 1) for i in range(cores)])

    u_mate = to_mate(velocity)
    piece = shape(snaps, comps, half, rows, span)
    pieces = call(piece_kernel, "piece", [piece] * (chips - 1))(velocity)
    got = [
        lax.ppermute(piece, "snap", [(i, (i + 2 * k) % cores) for i in range(cores)])
        for k, piece in zip(shifts, pieces)
    ]

    odd = z % 2 == 1
    levels = jnp.broadcast_to(jnp.pad(row_level, (0, span - rows)), (ROWS, span))
    mate_planes = half if chips == 2 else planes
    packed = shape(comps * (planes + mate_planes) + 1, ROWS, span)
    first, second = call(functools.partial(pack_kernel, mate_planes), "pack", [packed, packed])(
        levels, velocity, u_mate
    )

    def swap(array, first):
        pairs = []
        for i in range(spaces):
            j = ((i - first) ^ 1) + first
            alone = not 0 <= j < spaces
            pairs += [(i * cores + t, i * cores + (t ^ 1) if alone else j * cores + t) for t in range(cores)]
        return lax.ppermute(array, ("space", "snap"), pairs)

    first, second = swap(first, 0), swap(second, 1)
    factor = shape(planes, rows, span, dtype=F32)
    metric, volume = call(metric_kernel, "metric", [factor, factor])(levels, metric_table)
    operator = jnp.asarray(span_operator(span), BF16)
    scratch = [pltpu.VMEM((planes, rows + 2 * ROWS, span), F32)] * 2
    full = shape(*velocity.shape, dtype=F32)
    part, part_mate, energy = call(inner_kernel, "inner", [full, full, shape(snaps, rows, span, dtype=F32)], scratch)(
        velocity, u_mate, metric, volume, operator
    )
    first, second, part, *got = lax.optimization_barrier((first, second, part, *got))
    low = jnp.where(z > 0, jnp.where(odd, first, second), 0)
    high = jnp.where(z < spaces - 1, jnp.where(odd, second, first), 0)

    tile = shape(ROWS, span, dtype=F32)
    total, for_mate, back = 0, 0, []
    for k in shifts:
        answer = call(
            functools.partial(cross_kernel, k), "cross", [tile] * 3, [pltpu.VMEM((planes, 2, ROWS, span), F32)]
        )(metric_table, velocity, u_mate, part, part_mate, metric, low, high, got[k - 1])
        total = total + answer[0]
        for_mate = for_mate + answer[1]
        back.append(answer[2])
    w, gain = call(edge_kernel, "edges", [shape(*velocity.shape), shape(snaps, 2, ROWS, span, dtype=F32)])(
        metric_table, velocity, part, metric, low, high
    )
    total = total + call(functools.partial(square_kernel, False), "square", tile)(velocity, w)
    total = total + call(functools.partial(square_kernel, True), "mates", tile)(u_mate, w)
    profile = call(functools.partial(profile_kernel, planes), "profile", shape(snaps, rows, dtype=F32))(energy, gain)
    for k in shifts:
        total = total + lax.ppermute(back[k - 1], "snap", [(i, (i - 2 * k) % cores) for i in range(cores)])
    total = total + to_mate(for_mate)
    if spaces & (spaces - 1):
        gram = lax.psum(total, "space")
    else:
        gram = total
        step = 1
        while step < spaces:
            gram = gram + lax.ppermute(gram, "space", [(i, i ^ step) for i in range(spaces)])
            step *= 2
    gram = gram[:snaps, : snaps * cores] * (1.0 / (planes * rows * spaces * span))
    return gram, profile


def solution(mesh):
    in_specs = (P(("grp", "snap"), None, None, "space", None), P("space"), P())
    out_specs = (P(("grp", "snap"), None), P(("grp", "snap"), "space"))
    return jax.shard_map(local, mesh=mesh, in_specs=in_specs, out_specs=out_specs, check_vma=False)
```

```python
import functools

import jax
import jax.numpy as jnp
from jax import lax
from jax.experimental import pallas as pl
from jax.experimental.pallas import tpu as pltpu
from jax.sharding import PartitionSpec as P

F32 = jnp.float32
BF16 = jnp.bfloat16
ROWS = 8
VMEM = pl.BlockSpec(memory_space=pltpu.VMEM)


def call(kernel, name, out_shape, scratch_shapes=()):
    single = not isinstance(out_shape, list)

    def run(*args):
        return pl.pallas_call(
            kernel,
            name=name,
            out_shape=out_shape,
            in_specs=[VMEM] * len(args),
            out_specs=VMEM if single else [VMEM] * len(out_shape),
            scratch_shapes=list(scratch_shapes),
            compiler_params=pltpu.CompilerParams(vmem_limit_bytes=16 * 2**20),
            cost_estimate=pl.CostEstimate(flops=0, bytes_accessed=0, transcendentals=0),
        )(*args)

    return run


def sublane(shape):
    return lax.broadcasted_iota(jnp.int32, shape, len(shape) - 2)


def lanes(shape):
    return lax.broadcasted_iota(jnp.int32, shape, len(shape) - 1)


class Components:
    def __init__(self, refs):
        self.refs = refs

    def __getitem__(self, at):
        return self.refs[at[1]][(at[0],) + at[2:]]


def span_operator(cells):
    i, j = sublane((cells, cells)), lanes((cells, cells))
    low, high = jnp.maximum(i - 1, 0), jnp.minimum(i + 1, cells - 1)
    scale = jnp.where(high - low == 2, 0.25, 0.5)
    diff = jnp.where(j == high, scale, jnp.where(j == low, -scale, 0.0)).astype(BF16)
    return lax.dot_general(diff, diff, (((0,), (0,)), ((), ())), preferred_element_type=F32).astype(BF16)


def stretch_of(row_ids, rows):
    z, spaces = lax.axis_index("space"), lax.axis_size("space")
    return 0.25 + 2.25 * (row_ids + z * rows).astype(F32) / (rows * spaces - 1)


def half_here(k, planes):
    chips = lax.axis_size("snap") // 2
    chip = lax.axis_index("snap") // 2
    return jnp.where(chip < (chip + chips - k) % chips, 0, planes // 2)


def piece_kernel(u_ref, edge_ref, *refs):
    snaps, comps, planes, rows, span = u_ref.shape
    half = planes // 2
    pieces, components = refs[:-comps], refs[-comps:]
    chips = len(pieces) + 1
    chip = lax.axis_index("snap") // 2
    for k, piece in enumerate(pieces):
        start = jnp.where((chip + k + 1) % chips < chip, 0, half)
        for a in range(snaps):
            for c in range(comps):
                for i in range(half):
                    piece[a, c, i] = u_ref[a, c, start + i]
    for c in range(comps):
        components[c][...] = u_ref[:, c]
    row8 = sublane((ROWS, span))
    for t in range(comps * planes, edge_ref.shape[1]):
        edge_ref[0, t] = edge_ref[1, t] = jnp.zeros((ROWS, span), BF16)
    for c in range(comps):
        for p in range(planes):
            up = jnp.zeros((ROWS, span), F32)
            down = jnp.zeros((ROWS, span), F32)
            for a in range(snaps):
                mine = row8 // 2 == a
                first = u_ref[a, c, p, 0:ROWS, :].astype(F32)
                last = u_ref[a, c, p, rows - ROWS : rows, :].astype(F32)
                up = jnp.where(mine, pltpu.roll(last, (2 * a + 2) % ROWS, 0), up)
                down = jnp.where(mine, pltpu.roll(first, (2 * a) % ROWS, 0), down)
            edge_ref[0, c * planes + p] = up.astype(BF16)
            edge_ref[1, c * planes + p] = down.astype(BF16)


def pack_kernel(comps, planes, rows, table_ref, own_ref, mate_ref, first_ref, second_ref):
    count = comps * planes
    mate_planes = (first_ref.shape[0] - 1 - count) // comps
    span = first_ref.shape[2]
    row8, lane = sublane((ROWS, span)), lanes((1, table_ref.shape[1]))
    odd = lax.axis_index("space") % 2
    entries = []
    for j in (rows - 1, 0):
        level = jnp.sum(jnp.where(lane == j, table_ref[planes : planes + 1, :], 0.0), axis=1, keepdims=True)
        level = jnp.broadcast_to(level, (ROWS, span))
        high = jnp.floor(level * (1.0 / 128.0))
        entries.append(jnp.where(row8 == 0, high, jnp.where(row8 == 1, level - 128.0 * high, 1.0)))
    first_ref[first_ref.shape[0] - 1] = jnp.where(odd == 1, entries[1], entries[0]).astype(BF16)
    second_ref[first_ref.shape[0] - 1] = jnp.where(odd == 1, entries[0], entries[1]).astype(BF16)
    for ref, way in ((first_ref, odd), (second_ref, 1 - odd)):
        ref[0:count] = own_ref[way, 0:count]
        for c in range(comps):
            start = c * planes + (0 if mate_planes == planes else half_here(1, planes))
            at = count + c * mate_planes
            ref[at : at + mate_planes] = mate_ref[way, pl.ds(start, mate_planes)]


def metric_kernel(table_ref, metric_ref, volume_ref, operator_ref):
    planes, rows, span = metric_ref.shape
    levels = table_ref.shape[1]
    level = jnp.broadcast_to(table_ref[planes : planes + 1, 0:rows], (rows, rows))
    level = jnp.where(sublane((rows, rows)) == lanes((rows, rows)), level, 0.0)
    level = jnp.sum(level, axis=1, keepdims=True).astype(jnp.int32)
    chosen = jnp.broadcast_to(level, (rows, levels)) == lanes((rows, levels))
    stretch = stretch_of(sublane((rows, span)), rows)
    for p in range(planes):
        picked = jnp.sum(jnp.where(chosen, table_ref[p : p + 1, :], 0.0), axis=1, keepdims=True)
        picked = jnp.broadcast_to(picked, (rows, span))
        metric_ref[p] = picked / stretch
        volume_ref[p] = stretch / picked
    operator_ref[...] = span_operator(span)


def inner_kernel(comps, other, cores, *refs):
    sources = [Components(refs[i * comps : (i + 1) * comps]) for i in range(cores)]
    metric_ref, volume_ref, operator_ref, *parts, energy_ref, f_ref, e_ref = refs[cores * comps :]
    snaps, _, half, rows, span = parts[0].shape
    planes = 2 * half
    first, end = ROWS, ROWS + rows
    row = sublane((rows, span))
    within = (row > 0) & (row < rows - 1)
    for i in range(half):
        for ref in (f_ref, e_ref):
            ref[i, 0:first, :] = jnp.zeros((ROWS, span), F32)
            ref[i, end : end + ROWS, :] = jnp.zeros((ROWS, span), F32)

    def work(start, source, part_ref, own):
        def field(a, carry):
            total = jnp.zeros((rows, span), F32)
            for c in range(comps):
                raw = source[a, c][start : start + half]
                spanned = jnp.dot(raw.reshape(half * rows, span), operator_ref[...], preferred_element_type=F32)
                spanned = spanned.reshape(half, rows, span)
                u = {
                    p: source[a, c, p].astype(F32)
                    for p in range(max(start - 2, 0), min(start + half + 2, planes))
                }
                stream = {}
                for i in range(max(start - 1, 0), min(start + half + 1, planes)):
                    lo, hi = max(i - 1, 0), min(i + 1, planes - 1)
                    edge = (volume_ref[i] * (0.25 / (hi - lo) ** 2)) * (u[hi] - u[lo])
                    stream[hi] = stream[hi] + edge if hi in stream else edge
                    stream[lo] = stream[lo] - edge if lo in stream else -edge
                for i in range(half):
                    p = start + i
                    f_ref[i, first:end, :] = u[p]
                    jump = f_ref[i, first + 1 : end + 1, :] - f_ref[i, first - 1 : end - 1, :]
                    edge = jnp.where(within, (metric_ref[p] * 0.0625) * jump, 0.0)
                    e_ref[i, first:end, :] = edge
                    partial = volume_ref[p] * (u[p] + spanned[i]) + stream[p]
                    if own:
                        total = total + (u[p] * partial + edge * jump)
                    normal = e_ref[i, first - 1 : end - 1, :] - e_ref[i, first + 1 : end + 1, :]
                    part_ref[a, c, i] = partial + normal
            if own:
                energy_ref[a] = total
            return carry

        lax.fori_loop(0, snaps, field, 0)

    def both(start):
        for i in range(cores):
            work(start, sources[i], parts[i], i == 0)

    at_first = (half_here(1, planes) == 0) != other
    pl.when(at_first)(lambda: both(0))
    pl.when(jnp.logical_not(at_first))(lambda: both(half))


def edge_scales(table_ref, metric_ref, low_ref, high_ref):
    planes, rows, span = metric_ref.shape
    levels = table_ref.shape[1]
    row8 = sublane((ROWS, span))
    factors = []
    for ref, offset in ((low_ref, -1), (high_ref, rows)):
        sent = ref[ref.shape[0] - 1].astype(F32)
        level = (128.0 * sent[0:1, :] + sent[1:2, :]).astype(jnp.int32)
        chosen = lanes((planes, levels)) == jnp.broadcast_to(level[:, 0:1], (planes, levels))
        picked = jnp.sum(jnp.where(chosen, table_ref[0:planes, :], 0.0), axis=1, keepdims=True)
        stretch = stretch_of(jnp.full((1, span), offset, jnp.int32), rows)
        exists = sent[2:3, :] > 0.0
        factors.append(jnp.where(exists, jnp.broadcast_to(picked, (planes, span)) / stretch * 0.0625, 0.0))
    below, above = factors
    scales = []
    for p in range(planes):
        metric_low = metric_ref[p, 0:ROWS, :] * 0.0625
        metric_high = metric_ref[p, rows - ROWS : rows, :] * 0.0625
        scale_low = jnp.where(row8 == 0, jnp.broadcast_to(below[p : p + 1, :], (ROWS, span)), 0.0)
        scale_low = jnp.where(row8 == 1, pltpu.roll(metric_low, 1, 0), scale_low)
        scale_high = jnp.where(row8 == ROWS - 1, jnp.broadcast_to(above[p : p + 1, :], (ROWS, span)), 0.0)
        scale_high = jnp.where(row8 == ROWS - 2, pltpu.roll(metric_high, ROWS - 1, 0), scale_high)
        scales.append((scale_low, scale_high))
    return scales


def edges_at(scale, u, low, high, a):
    jump_low = u[0:ROWS] - pltpu.roll(low, (-2 * a) % ROWS, 0)
    jump_high = u[-ROWS:] - pltpu.roll(high, (ROWS - 2 - 2 * a) % ROWS, 0)
    edge_low, edge_high = scale[0] * jump_low, scale[1] * jump_high
    return edge_low, edge_high, edge_low * jump_low, edge_high * jump_high


def edge_kernel(table_ref, part_ref, other_ref, metric_ref, low_ref, high_ref, *refs):
    u_ref, (w_ref, gain_ref, scale_ref) = Components(refs[:-3]), refs[-3:]
    snaps, comps, planes, rows, span = w_ref.shape
    half = planes // 2
    for p, (low, high) in enumerate(edge_scales(table_ref, metric_ref, low_ref, high_ref)):
        scale_ref[p, 0] = low
        scale_ref[p, 1] = high
    start = half_here(1, planes)
    zero = jnp.zeros((ROWS, span), F32)
    sums = [[zero, zero] for _ in range(snaps)]
    for c in range(comps):
        for ref, begin in ((part_ref, start), (other_ref, half - start)):
            for i in range(half):
                p = begin + i
                scale = scale_ref[p, 0], scale_ref[p, 1]
                low, high = low_ref[c * planes + p].astype(F32), high_ref[c * planes + p].astype(F32)
                for a in range(snaps):
                    edges = edges_at(scale, u_ref[a, c, p].astype(F32), low, high, a)
                    sums[a] = [x + y for x, y in zip(sums[a], edges[2:])]
                    part = ref[a, c, i]
                    w_ref[a, c, p] = jnp.concatenate(
                        [part[0:ROWS] + edges[0], part[ROWS : rows - ROWS], part[rows - ROWS :] + edges[1]], axis=0
                    ).astype(BF16)
    for a in range(snaps):
        gain_ref[a, 0] = sums[a][0]
        gain_ref[a, 1] = sums[a][1]


def profile_kernel(planes, energy_ref, other_ref, gain_ref, profile_ref):
    snaps, rows, span = energy_ref.shape
    row8 = sublane((ROWS, span))
    ones = jnp.ones((ROWS, span), F32)
    for a in range(snaps):
        first = jnp.where(row8 == 0, pltpu.roll(gain_ref[a, 0], ROWS - 1, 0), 0.0)
        last = jnp.where(row8 == ROWS - 1, pltpu.roll(gain_ref[a, 1], 1, 0), 0.0)
        energy = energy_ref[a] + other_ref[a]
        energy = jnp.concatenate(
            [
                energy[0:ROWS] + first,
                energy[ROWS : rows - ROWS],
                energy[rows - ROWS :] + last,
            ],
            axis=0,
        )
        line = lax.dot_general(
            ones, energy, (((1,), (1,)), ((), ())), precision=lax.Precision.HIGHEST, preferred_element_type=F32
        )
        profile_ref[a : a + 1, :] = line[0:1, :] * (1.0 / (planes * span))


def pair_sums(sums, pairs, lefts, rights):
    lefts = [x.astype(F32) for x in lefts]
    rights = [x.astype(F32) for x in rights]
    out = list(sums)
    for t in range(0, lefts[0].shape[0], ROWS):
        for k, (a, b) in enumerate(pairs):
            out[k] = out[k] + lefts[a][t : t + ROWS] * rights[b][t : t + ROWS]
    return out


def totals(sums):
    tiles = []
    for start in range(0, len(sums), ROWS):
        tile = jnp.concatenate([jnp.sum(s, axis=0, keepdims=True) for s in sums[start : start + ROWS]], axis=0)
        tiles.append(jnp.broadcast_to(jnp.sum(tile, axis=1, keepdims=True), tile.shape))
    return tiles


def square_kernel(by_mate, *refs):
    w_ref, block_ref = refs[-2:]
    u_ref = Components(refs[:-2])
    snaps, comps, planes, rows, span = w_ref.shape
    row, lane = sublane((ROWS, span)), lanes((ROWS, span))
    pairs = [(b, a) for b in range(snaps) for a in range(snaps) if by_mate or a <= b]
    sums = [jnp.zeros((ROWS, span), F32) for _ in pairs]
    for c in range(comps):
        for p in range(planes):
            sums = pair_sums(
                sums, pairs, [u_ref[b, c, p] for b in range(snaps)], [w_ref[a, c, p] for a in range(snaps)]
            )
    core = lax.axis_index("snap")
    column = snaps * (core + 1 - 2 * (core % 2) if by_mate else core)
    block = jnp.zeros((ROWS, span), F32)
    stacked = []
    for b in range(snaps):
        stacked += [sums[pairs.index((b, a) if (b, a) in pairs else (a, b))] for a in range(snaps)]
        stacked += [sums[0]] * (ROWS - snaps)
    for b, tile in enumerate(totals(stacked)):
        block = jnp.where((lane == column + b) & (row < snaps), tile, block)
    block_ref[...] = block


def cross_kernel(
    k, table_ref, part_ref, mate_part_ref, metric_ref, low_ref, high_ref, got_ref, *refs
):
    own_ref, for_mate_ref, back_ref, scale_ref = refs[-4:]
    comps = part_ref.shape[1]
    u_ref, mate_ref = Components(refs[:comps]), Components(refs[comps:-4])
    snaps, comps, half, rows, span = got_ref.shape
    planes = 2 * half
    count = comps * planes
    group = ROWS // snaps
    mate_planes = (low_ref.shape[0] - 1 - count) // comps
    start = half_here(k, planes)
    for p, (low, high) in enumerate(edge_scales(table_ref, metric_ref, low_ref, high_ref)):
        scale_ref[p, 0] = low
        scale_ref[p, 1] = high
    lane, row = lanes((ROWS, span)), sublane((ROWS, span))
    pairs = [(i, j) for i in range(2 * snaps) for j in range(snaps)]
    sums = [jnp.zeros((ROWS, span), F32) for _ in pairs]
    for c in range(comps):
        for i in range(half):
            p = start + i
            scale = scale_ref[p, 0], scale_ref[p, 1]
            at_mate = count + c * mate_planes + (p if mate_planes == planes else i)
            left = []
            for u, part, at in ((u_ref, part_ref, c * planes + p), (mate_ref, mate_part_ref, at_mate)):
                low, high = low_ref[at].astype(F32), high_ref[at].astype(F32)
                for a in range(snaps):
                    edges = edges_at(scale, u[a, c, p].astype(F32), low, high, a)
                    w = part[a, c, i]
                    left.append(
                        jnp.concatenate(
                            [w[0:ROWS] + edges[0], w[ROWS : rows - ROWS], w[rows - ROWS :] + edges[1]], axis=0
                        )
                    )
            sums = pair_sums(sums, pairs, left, [got_ref[a, c, i] for a in range(snaps)])
    cores = lax.axis_size("snap")
    core = lax.axis_index("snap")
    own, mate = core * snaps, (core + 1 - 2 * (core % 2)) * snaps
    source = (core + cores - 2 * k) % cores * snaps
    ahead = jnp.zeros((ROWS, span), F32)
    flipped = [sums[i * snaps + j] for j in range(snaps) for i in range(2 * snaps)]
    for t, tile in enumerate(totals(flipped)):
        ahead = ahead + jnp.where(lane == source + t, tile, 0.0)
    own_ref[...] = jnp.where(row < snaps, ahead, 0.0)
    for_mate_ref[...] = jnp.where(row < snaps, pltpu.roll(ahead, ROWS - snaps, 0), 0.0)
    back = jnp.zeros((ROWS, span), F32)
    for t, tile in enumerate(totals(sums)):
        i = t * group + row // snaps
        back = back + jnp.where(lane == jnp.where(i < snaps, own + i, mate + i - snaps), tile, 0.0)
    fold = back
    for i in range(1, group):
        fold = fold + pltpu.roll(back, i * snaps, 0)
    back_ref[...] = fold


def local(velocity, row_level, metric_table):
    snaps, comps, planes, rows, span = velocity.shape
    spaces, cores = lax.axis_size("space"), lax.axis_size("snap")
    chips = cores // 2
    z = lax.axis_index("space")
    half = planes // 2
    shifts = range(1, chips)

    def shape(*dims, dtype=BF16):
        return jax.ShapeDtypeStruct(dims, dtype)

    def to_mate(array):
        return lax.ppermute(array, "snap", [(i, i ^ 1) for i in range(cores)])

    piece = shape(snaps, comps, half, rows, span)
    component = shape(snaps, planes, rows, span)
    tiles = max(comps * planes, snaps * planes * rows // ROWS // 2 + 1)
    edge_rows, *pieces = call(
        piece_kernel, "piece", [shape(2, tiles, ROWS, span)] + [piece] * (chips - 1) + [component] * comps
    )(velocity)
    u = pieces[chips - 1 :]
    edge_rows_mate = to_mate(edge_rows)
    u_mate = [to_mate(x) for x in u]
    got = [
        lax.ppermute(piece, "snap", [(i, (i + 2 * k) % cores) for i in range(cores)])
        for k, piece in zip(shifts, pieces[: chips - 1])
    ]

    odd = z % 2 == 1
    levels = max(metric_table.shape[1], rows)
    entries = jnp.pad(row_level[None, :], ((planes, ROWS - 1), (0, levels - rows))).astype(F32)
    table = jnp.pad(metric_table, ((0, ROWS), (0, levels - metric_table.shape[1]))) + entries
    factor = shape(planes, rows, span, dtype=F32)
    metric, volume, operator = call(metric_kernel, "metric", [factor, factor, shape(span, span)])(table)
    scratch = [pltpu.VMEM((half, rows + 2 * ROWS, span), F32)] * 2

    def inner(other, *velocities):
        parts = [shape(snaps, comps, half, rows, span, dtype=F32)] * len(velocities)
        return call(
            functools.partial(inner_kernel, comps, other, len(velocities)),
            "inner",
            parts + [shape(snaps, rows, span, dtype=F32)],
            scratch,
        )(*[x for velocity in velocities for x in velocity], metric, volume, operator)

    part, part_mate, energy = inner(False, u, u_mate)
    mate_planes = half if chips == 2 else planes
    packed = shape(comps * (planes + mate_planes) + 1, ROWS, span)
    first, second = call(functools.partial(pack_kernel, comps, planes, rows), "pack", [packed, packed])(
        table, edge_rows, edge_rows_mate
    )

    def swap(array, first):
        pairs = []
        for i in range(spaces):
            j = ((i - first) ^ 1) + first
            alone = not 0 <= j < spaces
            pairs += [(i * cores + t, i * cores + (t ^ 1) if alone else j * cores + t) for t in range(cores)]
        return lax.ppermute(array, ("space", "snap"), pairs)

    first, second = swap(first, 0), swap(second, 1)
    first, second, part, part_mate, *got = lax.optimization_barrier((first, second, part, part_mate, *got))
    low = jnp.where(z > 0, jnp.where(odd, first, second), 0)
    high = jnp.where(z < spaces - 1, jnp.where(odd, second, first), 0)

    tile = shape(ROWS, span, dtype=F32)
    total, for_mate, back = 0, 0, []
    chip = lax.axis_index("snap") // 2
    *others, energy_other = inner(True, *([u] if chips == 2 else [u, u_mate]))
    for k in shifts:
        parts = part, part_mate
        if k > 1:
            same = (chip < (chip + chips - k) % chips) == (chip < (chip + chips - 1) % chips)
            parts = [jnp.where(same, x, y) for x, y in zip(parts, others)]
        answer = call(
            functools.partial(cross_kernel, k), "cross", [tile] * 3, [pltpu.VMEM((planes, 2, ROWS, span), F32)]
        )(table, *parts, metric, low, high, got[k - 1], *u, *u_mate)
        total = total + answer[0]
        for_mate = for_mate + answer[1]
        back.append(answer[2])
    part_other = others[0]
    w, gain = call(
        edge_kernel,
        "edges",
        [shape(*velocity.shape), shape(snaps, 2, ROWS, span, dtype=F32)],
        [pltpu.VMEM((planes, 2, ROWS, span), F32)],
    )(table, part, part_other, metric, low, high, *u)
    total = total + call(functools.partial(square_kernel, False), "square", tile)(*u, w)
    total = total + call(functools.partial(square_kernel, True), "mates", tile)(*u_mate, w)
    profile = call(functools.partial(profile_kernel, planes), "profile", shape(snaps, rows, dtype=F32))(energy, energy_other, gain)
    for k in shifts:
        total = total + lax.ppermute(back[k - 1], "snap", [(i, (i - 2 * k) % cores) for i in range(cores)])
    total = total + to_mate(for_mate)
    if spaces & (spaces - 1):
        gram = lax.psum(total, "space")
    else:
        gram = total
        step = 1
        while step < spaces:
            gram = gram + lax.ppermute(gram, "space", [(i, i ^ step) for i in range(spaces)])
            step *= 2
    gram = gram[:snaps, : snaps * cores] * (1.0 / (planes * rows * spaces * span))
    return gram, profile


def solution(mesh):
    in_specs = (P(("grp", "snap"), None, None, "space", None), P("space"), P())
    out_specs = (P(("grp", "snap"), None), P(("grp", "snap"), "space"))
    return jax.shard_map(local, mesh=mesh, in_specs=in_specs, out_specs=out_specs, check_vma=False)
```

```python
import functools

import jax
import jax.numpy as jnp
from jax import lax
from jax.experimental import pallas as pl
from jax.experimental.pallas import tpu as pltpu
from jax.sharding import PartitionSpec as P

F32 = jnp.float32
BF16 = jnp.bfloat16
ROWS = 8
VMEM = pl.BlockSpec(memory_space=pltpu.VMEM)


def call(kernel, name, out_shape, scratch_shapes=()):
    single = not isinstance(out_shape, list)

    def run(*args):
        return pl.pallas_call(
            kernel,
            name=name,
            out_shape=out_shape,
            in_specs=[VMEM] * len(args),
            out_specs=VMEM if single else [VMEM] * len(out_shape),
            scratch_shapes=list(scratch_shapes),
            compiler_params=pltpu.CompilerParams(vmem_limit_bytes=16 * 2**20),
            cost_estimate=pl.CostEstimate(flops=0, bytes_accessed=0, transcendentals=0),
        )(*args)

    return run


def sublane(shape):
    return lax.broadcasted_iota(jnp.int32, shape, len(shape) - 2)


def lanes(shape):
    return lax.broadcasted_iota(jnp.int32, shape, len(shape) - 1)


class Components:
    def __init__(self, refs):
        self.refs = refs

    def __getitem__(self, at):
        return self.refs[at[1]][(at[0],) + at[2:]]


def span_operator(cells):
    i, j = sublane((cells, cells)), lanes((cells, cells))
    low, high = jnp.maximum(i - 1, 0), jnp.minimum(i + 1, cells - 1)
    scale = jnp.where(high - low == 2, 0.25, 0.5)
    diff = jnp.where(j == high, scale, jnp.where(j == low, -scale, 0.0)).astype(BF16)
    return lax.dot_general(diff, diff, (((0,), (0,)), ((), ())), preferred_element_type=F32).astype(BF16)


def stretch_of(row_ids, rows):
    z, spaces = lax.axis_index("space"), lax.axis_size("space")
    return 0.25 + 2.25 * (row_ids + z * rows).astype(F32) / (rows * spaces - 1)


def half_here(k, planes):
    chips = lax.axis_size("snap") // 2
    chip = lax.axis_index("snap") // 2
    return jnp.where(chip < (chip + chips - k) % chips, 0, planes // 2)


def piece_kernel(u_ref, edge_ref, *refs):
    snaps, comps, planes, rows, span = u_ref.shape
    half = planes // 2
    pieces, components = refs[:-comps], refs[-comps:]
    chips = len(pieces) + 1
    chip = lax.axis_index("snap") // 2
    for k, piece in enumerate(pieces):
        start = jnp.where((chip + k + 1) % chips < chip, 0, half)
        for a in range(snaps):
            for c in range(comps):
                for i in range(half):
                    piece[a, c, i] = u_ref[a, c, start + i]
    for c in range(comps):
        components[c][...] = u_ref[:, c]
    row8 = sublane((ROWS, span))
    for t in range(comps * planes, edge_ref.shape[1]):
        edge_ref[0, t] = edge_ref[1, t] = jnp.zeros((ROWS, span), BF16)
    for c in range(comps):
        for p in range(planes):
            up = jnp.zeros((ROWS, span), F32)
            down = jnp.zeros((ROWS, span), F32)
            for a in range(snaps):
                mine = row8 // 2 == a
                first = u_ref[a, c, p, 0:ROWS, :].astype(F32)
                last = u_ref[a, c, p, rows - ROWS : rows, :].astype(F32)
                up = jnp.where(mine, pltpu.roll(last, (2 * a + 2) % ROWS, 0), up)
                down = jnp.where(mine, pltpu.roll(first, (2 * a) % ROWS, 0), down)
            edge_ref[0, c * planes + p] = up.astype(BF16)
            edge_ref[1, c * planes + p] = down.astype(BF16)


def pack_kernel(comps, planes, rows, table_ref, own_ref, mate_ref, first_ref, second_ref):
    count = comps * planes
    mate_planes = (first_ref.shape[0] - 1 - count) // comps
    span = first_ref.shape[2]
    row8, lane = sublane((ROWS, span)), lanes((1, table_ref.shape[1]))
    odd = lax.axis_index("space") % 2
    entries = []
    for j in (rows - 1, 0):
        level = jnp.sum(jnp.where(lane == j, table_ref[planes : planes + 1, :], 0.0), axis=1, keepdims=True)
        level = jnp.broadcast_to(level, (ROWS, span))
        high = jnp.floor(level * (1.0 / 128.0))
        entries.append(jnp.where(row8 == 0, high, jnp.where(row8 == 1, level - 128.0 * high, 1.0)))
    first_ref[first_ref.shape[0] - 1] = jnp.where(odd == 1, entries[1], entries[0]).astype(BF16)
    second_ref[first_ref.shape[0] - 1] = jnp.where(odd == 1, entries[0], entries[1]).astype(BF16)
    for ref, way in ((first_ref, odd), (second_ref, 1 - odd)):
        ref[0:count] = own_ref[way, 0:count]
        for c in range(comps):
            start = c * planes + (0 if mate_planes == planes else half_here(1, planes))
            at = count + c * mate_planes
            ref[at : at + mate_planes] = mate_ref[way, pl.ds(start, mate_planes)]


def metric_kernel(table_ref, metric_ref, volume_ref, operator_ref):
    planes, rows, span = metric_ref.shape
    levels = table_ref.shape[1]
    level = jnp.broadcast_to(table_ref[planes : planes + 1, 0:rows], (rows, rows))
    level = jnp.where(sublane((rows, rows)) == lanes((rows, rows)), level, 0.0)
    level = jnp.sum(level, axis=1, keepdims=True).astype(jnp.int32)
    chosen = jnp.broadcast_to(level, (rows, levels)) == lanes((rows, levels))
    stretch = stretch_of(sublane((rows, span)), rows)
    for p in range(planes):
        picked = jnp.sum(jnp.where(chosen, table_ref[p : p + 1, :], 0.0), axis=1, keepdims=True)
        picked = jnp.broadcast_to(picked, (rows, span))
        metric_ref[p] = picked / stretch
        volume_ref[p] = stretch / picked
    operator_ref[...] = span_operator(span)


def inner_kernel(comps, other, cores, *refs):
    sources = [Components(refs[i * comps : (i + 1) * comps]) for i in range(cores)]
    metric_ref, volume_ref, operator_ref, *parts, energy_ref, f_ref, e_ref = refs[cores * comps :]
    snaps, _, half, rows, span = parts[0].shape
    planes = 2 * half
    first, end = ROWS, ROWS + rows
    row = sublane((rows, span))
    within = (row > 0) & (row < rows - 1)
    for i in range(half):
        for ref in (f_ref, e_ref):
            ref[i, 0:first, :] = jnp.zeros((ROWS, span), F32)
            ref[i, end : end + ROWS, :] = jnp.zeros((ROWS, span), F32)

    def work(start, source, part_ref, own):
        def field(a, carry):
            total = jnp.zeros((rows, span), F32)
            for c in range(comps):
                raw = source[a, c][start : start + half]
                spanned = jnp.dot(raw.reshape(half * rows, span), operator_ref[...], preferred_element_type=F32)
                spanned = spanned.reshape(half, rows, span)
                u = {
                    p: source[a, c, p].astype(F32)
                    for p in range(max(start - 2, 0), min(start + half + 2, planes))
                }
                stream = {}
                for i in range(max(start - 1, 0), min(start + half + 1, planes)):
                    lo, hi = max(i - 1, 0), min(i + 1, planes - 1)
                    edge = (volume_ref[i] * (0.25 / (hi - lo) ** 2)) * (u[hi] - u[lo])
                    stream[hi] = stream[hi] + edge if hi in stream else edge
                    stream[lo] = stream[lo] - edge if lo in stream else -edge
                for i in range(half):
                    p = start + i
                    f_ref[i, first:end, :] = u[p]
                    jump = f_ref[i, first + 1 : end + 1, :] - f_ref[i, first - 1 : end - 1, :]
                    edge = jnp.where(within, (metric_ref[p] * 0.0625) * jump, 0.0)
                    e_ref[i, first:end, :] = edge
                    partial = volume_ref[p] * (u[p] + spanned[i]) + stream[p]
                    if own:
                        total = total + (u[p] * partial + edge * jump)
                    normal = e_ref[i, first - 1 : end - 1, :] - e_ref[i, first + 1 : end + 1, :]
                    part_ref[a, c, i] = partial + normal
            if own:
                energy_ref[a] = total
            return carry

        lax.fori_loop(0, snaps, field, 0)

    def both(start):
        for i in range(cores):
            work(start, sources[i], parts[i], i == 0)

    at_first = (half_here(1, planes) == 0) != other
    pl.when(at_first)(lambda: both(0))
    pl.when(jnp.logical_not(at_first))(lambda: both(half))


def edge_scales(table_ref, metric_ref, low_ref, high_ref):
    planes, rows, span = metric_ref.shape
    levels = table_ref.shape[1]
    row8 = sublane((ROWS, span))
    factors = []
    for ref, offset in ((low_ref, -1), (high_ref, rows)):
        sent = ref[ref.shape[0] - 1].astype(F32)
        level = (128.0 * sent[0:1, :] + sent[1:2, :]).astype(jnp.int32)
        chosen = lanes((planes, levels)) == jnp.broadcast_to(level[:, 0:1], (planes, levels))
        picked = jnp.sum(jnp.where(chosen, table_ref[0:planes, :], 0.0), axis=1, keepdims=True)
        stretch = stretch_of(jnp.full((1, span), offset, jnp.int32), rows)
        exists = sent[2:3, :] > 0.0
        factors.append(jnp.where(exists, jnp.broadcast_to(picked, (planes, span)) / stretch * 0.0625, 0.0))
    below, above = factors
    scales = []
    for p in range(planes):
        metric_low = metric_ref[p, 0:ROWS, :] * 0.0625
        metric_high = metric_ref[p, rows - ROWS : rows, :] * 0.0625
        scale_low = jnp.where(row8 == 0, jnp.broadcast_to(below[p : p + 1, :], (ROWS, span)), 0.0)
        scale_low = jnp.where(row8 == 1, pltpu.roll(metric_low, 1, 0), scale_low)
        scale_high = jnp.where(row8 == ROWS - 1, jnp.broadcast_to(above[p : p + 1, :], (ROWS, span)), 0.0)
        scale_high = jnp.where(row8 == ROWS - 2, pltpu.roll(metric_high, ROWS - 1, 0), scale_high)
        scales.append((scale_low, scale_high))
    return scales


def edges_at(scale, u, low, high, a):
    jump_low = u[0:ROWS] - pltpu.roll(low, (-2 * a) % ROWS, 0)
    jump_high = u[-ROWS:] - pltpu.roll(high, (ROWS - 2 - 2 * a) % ROWS, 0)
    edge_low, edge_high = scale[0] * jump_low, scale[1] * jump_high
    return edge_low, edge_high, edge_low * jump_low, edge_high * jump_high


def edge_kernel(table_ref, part_ref, other_ref, metric_ref, low_ref, high_ref, *refs):
    u_ref, (w_ref, gain_ref, scale_ref) = Components(refs[:-3]), refs[-3:]
    snaps, comps, planes, rows, span = w_ref.shape
    half = planes // 2
    for p, (low, high) in enumerate(edge_scales(table_ref, metric_ref, low_ref, high_ref)):
        scale_ref[p, 0] = low
        scale_ref[p, 1] = high
    start = half_here(1, planes)
    zero = jnp.zeros((ROWS, span), F32)
    sums = [[zero, zero] for _ in range(snaps)]
    for c in range(comps):
        for ref, begin in ((part_ref, start), (other_ref, half - start)):
            for i in range(half):
                p = begin + i
                scale = scale_ref[p, 0], scale_ref[p, 1]
                low, high = low_ref[c * planes + p].astype(F32), high_ref[c * planes + p].astype(F32)
                for a in range(snaps):
                    edges = edges_at(scale, u_ref[a, c, p].astype(F32), low, high, a)
                    sums[a] = [x + y for x, y in zip(sums[a], edges[2:])]
                    part = ref[a, c, i]
                    w_ref[a, c, p] = jnp.concatenate(
                        [part[0:ROWS] + edges[0], part[ROWS : rows - ROWS], part[rows - ROWS :] + edges[1]], axis=0
                    ).astype(BF16)
    for a in range(snaps):
        gain_ref[a, 0] = sums[a][0]
        gain_ref[a, 1] = sums[a][1]


def profile_kernel(planes, energy_ref, other_ref, gain_ref, profile_ref):
    snaps, rows, span = energy_ref.shape
    row8 = sublane((ROWS, span))
    ones = jnp.ones((ROWS, span), F32)
    for a in range(snaps):
        first = jnp.where(row8 == 0, pltpu.roll(gain_ref[a, 0], ROWS - 1, 0), 0.0)
        last = jnp.where(row8 == ROWS - 1, pltpu.roll(gain_ref[a, 1], 1, 0), 0.0)
        energy = energy_ref[a] + other_ref[a]
        energy = jnp.concatenate(
            [
                energy[0:ROWS] + first,
                energy[ROWS : rows - ROWS],
                energy[rows - ROWS :] + last,
            ],
            axis=0,
        )
        line = lax.dot_general(
            ones, energy, (((1,), (1,)), ((), ())), precision=lax.Precision.HIGHEST, preferred_element_type=F32
        )
        profile_ref[a : a + 1, :] = line[0:1, :] * (1.0 / (planes * span))


def pair_sums(sums, pairs, lefts, rights):
    lefts = [x.astype(F32) for x in lefts]
    rights = [x.astype(F32) for x in rights]
    out = list(sums)
    for t in range(0, lefts[0].shape[0], ROWS):
        for k, (a, b) in enumerate(pairs):
            out[k] = out[k] + lefts[a][t : t + ROWS] * rights[b][t : t + ROWS]
    return out


def totals(sums):
    tiles = []
    for start in range(0, len(sums), ROWS):
        tile = jnp.concatenate([jnp.sum(s, axis=0, keepdims=True) for s in sums[start : start + ROWS]], axis=0)
        tiles.append(jnp.broadcast_to(jnp.sum(tile, axis=1, keepdims=True), tile.shape))
    return tiles


def square_kernel(by_mate, *refs):
    w_ref, block_ref = refs[-2:]
    u_ref = Components(refs[:-2])
    snaps, comps, planes, rows, span = w_ref.shape
    row, lane = sublane((ROWS, span)), lanes((ROWS, span))
    pairs = [(b, a) for b in range(snaps) for a in range(snaps) if by_mate or a <= b]
    sums = [jnp.zeros((ROWS, span), F32) for _ in pairs]
    for c in range(comps):
        for p in range(planes):
            sums = pair_sums(
                sums, pairs, [u_ref[b, c, p] for b in range(snaps)], [w_ref[a, c, p] for a in range(snaps)]
            )
    core = lax.axis_index("snap")
    column = snaps * (core + 1 - 2 * (core % 2) if by_mate else core)
    block = jnp.zeros((ROWS, span), F32)
    stacked = []
    for b in range(snaps):
        stacked += [sums[pairs.index((b, a) if (b, a) in pairs else (a, b))] for a in range(snaps)]
        stacked += [sums[0]] * (ROWS - snaps)
    for b, tile in enumerate(totals(stacked)):
        block = jnp.where((lane == column + b) & (row < snaps), tile, block)
    block_ref[...] = block


def cross_kernel(
    k, table_ref, part_ref, mate_part_ref, metric_ref, low_ref, high_ref, got_ref, *refs
):
    own_ref, for_mate_ref, back_ref, scale_ref = refs[-4:]
    comps = part_ref.shape[1]
    u_ref, mate_ref = Components(refs[:comps]), Components(refs[comps:-4])
    snaps, comps, half, rows, span = got_ref.shape
    planes = 2 * half
    count = comps * planes
    group = ROWS // snaps
    mate_planes = (low_ref.shape[0] - 1 - count) // comps
    start = half_here(k, planes)
    for p, (low, high) in enumerate(edge_scales(table_ref, metric_ref, low_ref, high_ref)):
        scale_ref[p, 0] = low
        scale_ref[p, 1] = high
    lane, row = lanes((ROWS, span)), sublane((ROWS, span))
    pairs = [(i, j) for i in range(2 * snaps) for j in range(snaps)]
    sums = [jnp.zeros((ROWS, span), F32) for _ in pairs]
    for c in range(comps):
        for i in range(half):
            p = start + i
            scale = scale_ref[p, 0], scale_ref[p, 1]
            at_mate = count + c * mate_planes + (p if mate_planes == planes else i)
            left = []
            for u, part, at in ((u_ref, part_ref, c * planes + p), (mate_ref, mate_part_ref, at_mate)):
                low, high = low_ref[at].astype(F32), high_ref[at].astype(F32)
                for a in range(snaps):
                    edges = edges_at(scale, u[a, c, p].astype(F32), low, high, a)
                    w = part[a, c, i]
                    left.append(
                        jnp.concatenate(
                            [w[0:ROWS] + edges[0], w[ROWS : rows - ROWS], w[rows - ROWS :] + edges[1]], axis=0
                        )
                    )
            sums = pair_sums(sums, pairs, left, [got_ref[a, c, i] for a in range(snaps)])
    cores = lax.axis_size("snap")
    core = lax.axis_index("snap")
    own, mate = core * snaps, (core + 1 - 2 * (core % 2)) * snaps
    source = (core + cores - 2 * k) % cores * snaps
    ahead = jnp.zeros((ROWS, span), F32)
    flipped = [sums[i * snaps + j] for j in range(snaps) for i in range(2 * snaps)]
    for t, tile in enumerate(totals(flipped)):
        ahead = ahead + jnp.where(lane == source + t, tile, 0.0)
    own_ref[...] = jnp.where(row < snaps, ahead, 0.0)
    for_mate_ref[...] = jnp.where(row < snaps, pltpu.roll(ahead, ROWS - snaps, 0), 0.0)
    back = jnp.zeros((ROWS, span), F32)
    for t, tile in enumerate(totals(sums)):
        i = t * group + row // snaps
        back = back + jnp.where(lane == jnp.where(i < snaps, own + i, mate + i - snaps), tile, 0.0)
    fold = back
    for i in range(1, group):
        fold = fold + pltpu.roll(back, i * snaps, 0)
    back_ref[...] = fold


def local(velocity, row_level, metric_table):
    snaps, comps, planes, rows, span = velocity.shape
    spaces, cores = lax.axis_size("space"), lax.axis_size("snap")
    chips = cores // 2
    z = lax.axis_index("space")
    half = planes // 2
    shifts = range(1, chips)

    def shape(*dims, dtype=BF16):
        return jax.ShapeDtypeStruct(dims, dtype)

    def to_mate(array):
        return lax.ppermute(array, "snap", [(i, i ^ 1) for i in range(cores)])

    piece = shape(snaps, comps, half, rows, span)
    component = shape(snaps, planes, rows, span)
    tiles = max(comps * planes, snaps * planes * rows // ROWS // 2 + 1)
    edge_rows, *pieces = call(
        piece_kernel, "piece", [shape(2, tiles, ROWS, span)] + [piece] * (chips - 1) + [component] * comps
    )(velocity)
    u = pieces[chips - 1 :]
    edge_rows_mate = to_mate(edge_rows)
    u_mate = [to_mate(x) for x in u]
    got = [
        lax.ppermute(piece, "snap", [(i, (i + 2 * k) % cores) for i in range(cores)])
        for k, piece in zip(shifts, pieces[: chips - 1])
    ]

    odd = z % 2 == 1
    levels = max(metric_table.shape[1], rows)
    entries = jnp.pad(row_level[None, :], ((planes, ROWS - 1), (0, levels - rows))).astype(F32)
    table = jnp.pad(metric_table, ((0, ROWS), (0, levels - metric_table.shape[1]))) + entries
    factor = shape(planes, rows, span, dtype=F32)
    metric, volume, operator = call(metric_kernel, "metric", [factor, factor, shape(span, span)])(table)
    scratch = [pltpu.VMEM((half, rows + 2 * ROWS, span), F32)] * 2

    def inner(other, *velocities):
        parts = [shape(snaps, comps, half, rows, span, dtype=F32)] * len(velocities)
        return call(
            functools.partial(inner_kernel, comps, other, len(velocities)),
            "inner",
            parts + [shape(snaps, rows, span, dtype=F32)],
            scratch,
        )(*[x for velocity in velocities for x in velocity], metric, volume, operator)

    part, part_mate, energy = inner(False, u, u_mate)
    mate_planes = half if chips == 2 else planes
    packed = shape(comps * (planes + mate_planes) + 1, ROWS, span)
    first, second = call(functools.partial(pack_kernel, comps, planes, rows), "pack", [packed, packed])(
        table, edge_rows, edge_rows_mate
    )

    def swap(array, first):
        pairs = []
        for i in range(spaces):
            j = ((i - first) ^ 1) + first
            alone = not 0 <= j < spaces
            pairs += [(i * cores + t, i * cores + (t ^ 1) if alone else j * cores + t) for t in range(cores)]
        return lax.ppermute(array, ("space", "snap"), pairs)

    first, second = swap(first, 0), swap(second, 1)
    first, second, part, part_mate, *got = lax.optimization_barrier((first, second, part, part_mate, *got))
    low = jnp.where(z > 0, jnp.where(odd, first, second), 0)
    high = jnp.where(z < spaces - 1, jnp.where(odd, second, first), 0)

    tile = shape(ROWS, span, dtype=F32)
    total, for_mate, back = 0, 0, []
    chip = lax.axis_index("snap") // 2
    *others, energy_other = inner(True, *([u] if chips == 2 else [u, u_mate]))
    for k in shifts:
        parts = part, part_mate
        if k > 1:
            same = (chip < (chip + chips - k) % chips) == (chip < (chip + chips - 1) % chips)
            parts = [jnp.where(same, x, y) for x, y in zip(parts, others)]
        answer = call(
            functools.partial(cross_kernel, k), "cross", [tile] * 3, [pltpu.VMEM((planes, 2, ROWS, span), F32)]
        )(table, *parts, metric, low, high, got[k - 1], *u, *u_mate)
        total = total + answer[0]
        for_mate = for_mate + answer[1]
        back.append(answer[2])
    part_other = others[0]
    w, gain = call(
        edge_kernel,
        "edges",
        [shape(*velocity.shape), shape(snaps, 2, ROWS, span, dtype=F32)],
        [pltpu.VMEM((planes, 2, ROWS, span), F32)],
    )(table, part, part_other, metric, low, high, *u)
    total = total + call(functools.partial(square_kernel, False), "square", tile)(*u, w)
    total = total + call(functools.partial(square_kernel, True), "mates", tile)(*u_mate, w)
    profile = call(functools.partial(profile_kernel, planes), "profile", shape(snaps, rows, dtype=F32))(energy, energy_other, gain)
    for k in shifts:
        total = total + lax.ppermute(back[k - 1], "snap", [(i, (i - 2 * k) % cores) for i in range(cores)])
    total = total + to_mate(for_mate)
    if spaces & (spaces - 1):
        gram = lax.psum(total, "space")
    else:
        gram = total
        step = spaces // 2
        while step:
            gram = gram + lax.ppermute(gram, "space", [(i, i ^ step) for i in range(spaces)])
            step //= 2
    gram = gram[:snaps, : snaps * cores] * (1.0 / (planes * rows * spaces * span))
    return gram, profile


def solution(mesh):
    in_specs = (P(("grp", "snap"), None, None, "space", None), P("space"), P())
    out_specs = (P(("grp", "snap"), None), P(("grp", "snap"), "space"))
    return jax.shard_map(local, mesh=mesh, in_specs=in_specs, out_specs=out_specs, check_vma=False)
```

```python
import functools

import jax
import jax.numpy as jnp
from jax import lax
from jax.experimental import pallas as pl
from jax.experimental.pallas import tpu as pltpu
from jax.sharding import PartitionSpec as P

F32 = jnp.float32
BF16 = jnp.bfloat16
ROWS = 8
VMEM = pl.BlockSpec(memory_space=pltpu.VMEM)


def call(kernel, name, out_shape, scratch_shapes=()):
    single = not isinstance(out_shape, list)

    def run(*args):
        return pl.pallas_call(
            kernel,
            name=name,
            out_shape=out_shape,
            in_specs=[VMEM] * len(args),
            out_specs=VMEM if single else [VMEM] * len(out_shape),
            scratch_shapes=list(scratch_shapes),
            compiler_params=pltpu.CompilerParams(vmem_limit_bytes=16 * 2**20),
            cost_estimate=pl.CostEstimate(flops=0, bytes_accessed=0, transcendentals=0),
        )(*args)

    return run


def sublane(shape):
    return lax.broadcasted_iota(jnp.int32, shape, len(shape) - 2)


def lanes(shape):
    return lax.broadcasted_iota(jnp.int32, shape, len(shape) - 1)


class Components:
    def __init__(self, refs):
        self.refs = refs

    def __getitem__(self, at):
        return self.refs[at[1]][(at[0],) + at[2:]]


def span_operator(cells):
    i, j = sublane((cells, cells)), lanes((cells, cells))
    low, high = jnp.maximum(i - 1, 0), jnp.minimum(i + 1, cells - 1)
    scale = jnp.where(high - low == 2, 0.25, 0.5)
    diff = jnp.where(j == high, scale, jnp.where(j == low, -scale, 0.0)).astype(BF16)
    return lax.dot_general(diff, diff, (((0,), (0,)), ((), ())), preferred_element_type=F32).astype(BF16)


def stretch_of(row_ids, rows):
    z, spaces = lax.axis_index("space"), lax.axis_size("space")
    return 0.25 + 2.25 * (row_ids + z * rows).astype(F32) / (rows * spaces - 1)


def half_here(k, planes):
    chips = lax.axis_size("snap") // 2
    chip = lax.axis_index("snap") // 2
    return jnp.where(chip < (chip + chips - k) % chips, 0, planes // 2)


def piece_kernel(u_ref, edge_ref, *refs):
    snaps, comps, planes, rows, span = u_ref.shape
    half = planes // 2
    pieces, components = refs[:-comps], refs[-comps:]
    chips = len(pieces) + 1
    chip = lax.axis_index("snap") // 2
    for k, piece in enumerate(pieces):
        start = jnp.where((chip + k + 1) % chips < chip, 0, half - 1)
        for a in range(snaps):
            for c in range(comps):
                for i in range(half + 1):
                    piece[a, c, i] = u_ref[a, c, start + i]
    for c in range(comps):
        components[c][...] = u_ref[:, c]
    row8 = sublane((ROWS, span))
    for t in range(comps * planes, edge_ref.shape[1]):
        edge_ref[0, t] = edge_ref[1, t] = jnp.zeros((ROWS, span), BF16)
    for c in range(comps):
        for p in range(planes):
            up = jnp.zeros((ROWS, span), F32)
            down = jnp.zeros((ROWS, span), F32)
            for a in range(snaps):
                mine = row8 // 2 == a
                first = u_ref[a, c, p, 0:ROWS, :].astype(F32)
                last = u_ref[a, c, p, rows - ROWS : rows, :].astype(F32)
                up = jnp.where(mine, pltpu.roll(last, (2 * a + 2) % ROWS, 0), up)
                down = jnp.where(mine, pltpu.roll(first, (2 * a) % ROWS, 0), down)
            edge_ref[0, c * planes + p] = up.astype(BF16)
            edge_ref[1, c * planes + p] = down.astype(BF16)


def pack_kernel(comps, planes, rows, table_ref, own_ref, mate_ref, first_ref, second_ref):
    count = comps * planes
    mate_planes = (first_ref.shape[0] - 1 - count) // comps
    span = first_ref.shape[2]
    row8, lane = sublane((ROWS, span)), lanes((1, table_ref.shape[1]))
    odd = lax.axis_index("space") % 2
    entries = []
    for j in (rows - 1, 0):
        level = jnp.sum(jnp.where(lane == j, table_ref[planes : planes + 1, :], 0.0), axis=1, keepdims=True)
        level = jnp.broadcast_to(level, (ROWS, span))
        high = jnp.floor(level * (1.0 / 128.0))
        entries.append(jnp.where(row8 == 0, high, jnp.where(row8 == 1, level - 128.0 * high, 1.0)))
    first_ref[first_ref.shape[0] - 1] = jnp.where(odd == 1, entries[1], entries[0]).astype(BF16)
    second_ref[first_ref.shape[0] - 1] = jnp.where(odd == 1, entries[0], entries[1]).astype(BF16)
    for ref, way in ((first_ref, odd), (second_ref, 1 - odd)):
        ref[0:count] = own_ref[way, 0:count]
        for c in range(comps):
            start = c * planes + (0 if mate_planes == planes else half_here(1, planes))
            at = count + c * mate_planes
            ref[at : at + mate_planes] = mate_ref[way, pl.ds(start, mate_planes)]


def metric_kernel(table_ref, metric_ref, volume_ref, operator_ref):
    planes, rows, span = metric_ref.shape
    levels = table_ref.shape[1]
    level = jnp.broadcast_to(table_ref[planes : planes + 1, 0:rows], (rows, rows))
    level = jnp.where(sublane((rows, rows)) == lanes((rows, rows)), level, 0.0)
    level = jnp.sum(level, axis=1, keepdims=True).astype(jnp.int32)
    chosen = jnp.broadcast_to(level, (rows, levels)) == lanes((rows, levels))
    stretch = stretch_of(sublane((rows, span)), rows)
    for p in range(planes):
        picked = jnp.sum(jnp.where(chosen, table_ref[p : p + 1, :], 0.0), axis=1, keepdims=True)
        picked = jnp.broadcast_to(picked, (rows, span))
        metric_ref[p] = picked / stretch
        volume_ref[p] = stretch / picked
    operator_ref[...] = span_operator(span)


def inner_kernel(comps, other, cores, *refs):
    sources = [Components(refs[i * comps : (i + 1) * comps]) for i in range(cores)]
    metric_ref, volume_ref, operator_ref, *parts, energy_ref, f_ref, e_ref = refs[cores * comps :]
    snaps, _, half, rows, span = parts[0].shape
    half -= 1
    planes = 2 * half
    first, end = ROWS, ROWS + rows
    row = sublane((rows, span))
    within = (row > 0) & (row < rows - 1)
    for i in range(half):
        for ref in (f_ref, e_ref):
            ref[i, 0:first, :] = jnp.zeros((ROWS, span), F32)
            ref[i, end : end + ROWS, :] = jnp.zeros((ROWS, span), F32)

    def work(start, source, part_ref, own):
        def field(a, carry):
            total = jnp.zeros((rows, span), F32)
            for c in range(comps):
                raw = source[a, c][start : start + half]
                spanned = jnp.dot(raw.reshape(half * rows, span), operator_ref[...], preferred_element_type=F32)
                spanned = spanned.reshape(half, rows, span)
                begin = max(start - 1, 0)
                u = {p: source[a, c, p].astype(F32) for p in range(begin, begin + half + 1)}
                stream = {}
                for i in range(start, start + half):
                    lo, hi = max(i - 1, 0), min(i + 1, planes - 1)
                    edge = (volume_ref[i] * (0.25 / (hi - lo) ** 2)) * (u[hi] - u[lo])
                    stream[hi] = stream[hi] + edge if hi in stream else edge
                    stream[lo] = stream[lo] - edge if lo in stream else -edge
                for i in range(half):
                    p = start + i
                    f_ref[i, first:end, :] = u[p]
                    jump = f_ref[i, first + 1 : end + 1, :] - f_ref[i, first - 1 : end - 1, :]
                    edge = jnp.where(within, (metric_ref[p] * 0.0625) * jump, 0.0)
                    e_ref[i, first:end, :] = edge
                    partial = volume_ref[p] * (u[p] + spanned[i]) + stream[p]
                    if own:
                        total = total + (u[p] * partial + edge * jump)
                    normal = e_ref[i, first - 1 : end - 1, :] - e_ref[i, first + 1 : end + 1, :]
                    part_ref[a, c, p - begin] = partial + normal
                (beyond,) = [p for p in u if not start <= p < start + half]
                part_ref[a, c, beyond - begin] = stream[beyond]
                if own:
                    total = total + u[beyond] * stream[beyond]
            if own:
                energy_ref[a] = total
            return carry

        lax.fori_loop(0, snaps, field, 0)

    def both(start):
        for i in range(cores):
            work(start, sources[i], parts[i], i == 0)

    at_first = (half_here(1, planes) == 0) != other
    pl.when(at_first)(lambda: both(0))
    pl.when(jnp.logical_not(at_first))(lambda: both(half))


def edge_scales(table_ref, metric_ref, low_ref, high_ref):
    planes, rows, span = metric_ref.shape
    levels = table_ref.shape[1]
    row8 = sublane((ROWS, span))
    factors = []
    for ref, offset in ((low_ref, -1), (high_ref, rows)):
        sent = ref[ref.shape[0] - 1].astype(F32)
        level = (128.0 * sent[0:1, :] + sent[1:2, :]).astype(jnp.int32)
        chosen = lanes((planes, levels)) == jnp.broadcast_to(level[:, 0:1], (planes, levels))
        picked = jnp.sum(jnp.where(chosen, table_ref[0:planes, :], 0.0), axis=1, keepdims=True)
        stretch = stretch_of(jnp.full((1, span), offset, jnp.int32), rows)
        exists = sent[2:3, :] > 0.0
        factors.append(jnp.where(exists, jnp.broadcast_to(picked, (planes, span)) / stretch * 0.0625, 0.0))
    below, above = factors
    scales = []
    for p in range(planes):
        metric_low = metric_ref[p, 0:ROWS, :] * 0.0625
        metric_high = metric_ref[p, rows - ROWS : rows, :] * 0.0625
        scale_low = jnp.where(row8 == 0, jnp.broadcast_to(below[p : p + 1, :], (ROWS, span)), 0.0)
        scale_low = jnp.where(row8 == 1, pltpu.roll(metric_low, 1, 0), scale_low)
        scale_high = jnp.where(row8 == ROWS - 1, jnp.broadcast_to(above[p : p + 1, :], (ROWS, span)), 0.0)
        scale_high = jnp.where(row8 == ROWS - 2, pltpu.roll(metric_high, ROWS - 1, 0), scale_high)
        scales.append((scale_low, scale_high))
    return scales


def edges_at(scale, u, low, high, a):
    jump_low = u[0:ROWS] - pltpu.roll(low, (-2 * a) % ROWS, 0)
    jump_high = u[-ROWS:] - pltpu.roll(high, (ROWS - 2 - 2 * a) % ROWS, 0)
    edge_low, edge_high = scale[0] * jump_low, scale[1] * jump_high
    return edge_low, edge_high, edge_low * jump_low, edge_high * jump_high


def edge_kernel(table_ref, part_ref, other_ref, metric_ref, low_ref, high_ref, *refs):
    u_ref, (w_ref, gain_ref, scale_ref) = Components(refs[:-3]), refs[-3:]
    snaps, comps, planes, rows, span = w_ref.shape
    half = planes // 2
    for p, (low, high) in enumerate(edge_scales(table_ref, metric_ref, low_ref, high_ref)):
        scale_ref[p, 0] = low
        scale_ref[p, 1] = high
    start = half_here(1, planes)
    zero = jnp.zeros((ROWS, span), F32)
    sums = [[zero, zero] for _ in range(snaps)]
    for c in range(comps):
        for ref, beside, begin in ((part_ref, other_ref, start), (other_ref, part_ref, half - start)):
            first = begin == 0
            for i in range(half):
                p = begin + i
                scale = scale_ref[p, 0], scale_ref[p, 1]
                low, high = low_ref[c * planes + p].astype(F32), high_ref[c * planes + p].astype(F32)
                for a in range(snaps):
                    edges = edges_at(scale, u_ref[a, c, p].astype(F32), low, high, a)
                    sums[a] = [x + y for x, y in zip(sums[a], edges[2:])]
                    part = ref[a, c, i + jnp.where(first, 0, 1)]
                    if i == 0:
                        part = part + jnp.where(first, 0.0, beside[a, c, half])
                    if i == half - 1:
                        part = part + jnp.where(first, beside[a, c, 0], 0.0)
                    w_ref[a, c, p] = jnp.concatenate(
                        [part[0:ROWS] + edges[0], part[ROWS : rows - ROWS], part[rows - ROWS :] + edges[1]], axis=0
                    ).astype(BF16)
    for a in range(snaps):
        gain_ref[a, 0] = sums[a][0]
        gain_ref[a, 1] = sums[a][1]


def profile_kernel(planes, energy_ref, other_ref, gain_ref, profile_ref):
    snaps, rows, span = energy_ref.shape
    row8 = sublane((ROWS, span))
    ones = jnp.ones((ROWS, span), F32)
    for a in range(snaps):
        first = jnp.where(row8 == 0, pltpu.roll(gain_ref[a, 0], ROWS - 1, 0), 0.0)
        last = jnp.where(row8 == ROWS - 1, pltpu.roll(gain_ref[a, 1], 1, 0), 0.0)
        energy = energy_ref[a] + other_ref[a]
        energy = jnp.concatenate(
            [
                energy[0:ROWS] + first,
                energy[ROWS : rows - ROWS],
                energy[rows - ROWS :] + last,
            ],
            axis=0,
        )
        line = lax.dot_general(
            ones, energy, (((1,), (1,)), ((), ())), precision=lax.Precision.HIGHEST, preferred_element_type=F32
        )
        profile_ref[a : a + 1, :] = line[0:1, :] * (1.0 / (planes * span))


def pair_sums(sums, pairs, lefts, rights):
    lefts = [x.astype(F32) for x in lefts]
    rights = [x.astype(F32) for x in rights]
    out = list(sums)
    for t in range(0, lefts[0].shape[0], ROWS):
        for k, (a, b) in enumerate(pairs):
            out[k] = out[k] + lefts[a][t : t + ROWS] * rights[b][t : t + ROWS]
    return out


def totals(sums):
    tiles = []
    for start in range(0, len(sums), ROWS):
        tile = jnp.concatenate([jnp.sum(s, axis=0, keepdims=True) for s in sums[start : start + ROWS]], axis=0)
        tiles.append(jnp.broadcast_to(jnp.sum(tile, axis=1, keepdims=True), tile.shape))
    return tiles


def square_kernel(by_mate, *refs):
    w_ref, block_ref = refs[-2:]
    u_ref = Components(refs[:-2])
    snaps, comps, planes, rows, span = w_ref.shape
    row, lane = sublane((ROWS, span)), lanes((ROWS, span))
    pairs = [(b, a) for b in range(snaps) for a in range(snaps) if by_mate or a <= b]
    sums = [jnp.zeros((ROWS, span), F32) for _ in pairs]
    for c in range(comps):
        for p in range(planes):
            sums = pair_sums(
                sums, pairs, [u_ref[b, c, p] for b in range(snaps)], [w_ref[a, c, p] for a in range(snaps)]
            )
    core = lax.axis_index("snap")
    column = snaps * (core + 1 - 2 * (core % 2) if by_mate else core)
    block = jnp.zeros((ROWS, span), F32)
    stacked = []
    for b in range(snaps):
        stacked += [sums[pairs.index((b, a) if (b, a) in pairs else (a, b))] for a in range(snaps)]
        stacked += [sums[0]] * (ROWS - snaps)
    for b, tile in enumerate(totals(stacked)):
        block = jnp.where((lane == column + b) & (row < snaps), tile, block)
    block_ref[...] = block


def cross_kernel(
    k, table_ref, part_ref, mate_part_ref, metric_ref, low_ref, high_ref, got_ref, *refs
):
    own_ref, for_mate_ref, back_ref, scale_ref = refs[-4:]
    comps = part_ref.shape[1]
    u_ref, mate_ref = Components(refs[:comps]), Components(refs[comps:-4])
    snaps, comps, half, rows, span = got_ref.shape
    half -= 1
    planes = 2 * half
    count = comps * planes
    group = ROWS // snaps
    mate_planes = (low_ref.shape[0] - 1 - count) // comps
    start = half_here(k, planes)
    for p, (low, high) in enumerate(edge_scales(table_ref, metric_ref, low_ref, high_ref)):
        scale_ref[p, 0] = low
        scale_ref[p, 1] = high
    lane, row = lanes((ROWS, span)), sublane((ROWS, span))
    pairs = [(i, j) for i in range(2 * snaps) for j in range(snaps)]
    sums = [jnp.zeros((ROWS, span), F32) for _ in pairs]
    for c in range(comps):
        for i in range(half + 1):
            p = jnp.where(start == 0, 0, half - 1) + i
            scale = scale_ref[p, 0], scale_ref[p, 1]
            if i in (0, half):
                inside = (start == 0) == (i == 0)
                scale = [jnp.where(inside, x, 0.0) for x in scale]
            at = p if mate_planes == planes else jnp.clip(p - start, 0, half - 1)
            at_mate = count + c * mate_planes + at
            left = []
            for u, part, at in ((u_ref, part_ref, c * planes + p), (mate_ref, mate_part_ref, at_mate)):
                low, high = low_ref[at].astype(F32), high_ref[at].astype(F32)
                for a in range(snaps):
                    edges = edges_at(scale, u[a, c, p].astype(F32), low, high, a)
                    w = part[a, c, i]
                    left.append(
                        jnp.concatenate(
                            [w[0:ROWS] + edges[0], w[ROWS : rows - ROWS], w[rows - ROWS :] + edges[1]], axis=0
                        )
                    )
            sums = pair_sums(sums, pairs, left, [got_ref[a, c, i] for a in range(snaps)])
    cores = lax.axis_size("snap")
    core = lax.axis_index("snap")
    own, mate = core * snaps, (core + 1 - 2 * (core % 2)) * snaps
    source = (core + cores - 2 * k) % cores * snaps
    ahead = jnp.zeros((ROWS, span), F32)
    flipped = [sums[i * snaps + j] for j in range(snaps) for i in range(2 * snaps)]
    for t, tile in enumerate(totals(flipped)):
        ahead = ahead + jnp.where(lane == source + t, tile, 0.0)
    own_ref[...] = jnp.where(row < snaps, ahead, 0.0)
    for_mate_ref[...] = jnp.where(row < snaps, pltpu.roll(ahead, ROWS - snaps, 0), 0.0)
    back = jnp.zeros((ROWS, span), F32)
    for t, tile in enumerate(totals(sums)):
        i = t * group + row // snaps
        back = back + jnp.where(lane == jnp.where(i < snaps, own + i, mate + i - snaps), tile, 0.0)
    fold = back
    for i in range(1, group):
        fold = fold + pltpu.roll(back, i * snaps, 0)
    back_ref[...] = fold


def local(velocity, row_level, metric_table):
    snaps, comps, planes, rows, span = velocity.shape
    spaces, cores = lax.axis_size("space"), lax.axis_size("snap")
    chips = cores // 2
    z = lax.axis_index("space")
    half = planes // 2
    shifts = range(1, chips)

    def shape(*dims, dtype=BF16):
        return jax.ShapeDtypeStruct(dims, dtype)

    def to_mate(array):
        return lax.ppermute(array, "snap", [(i, i ^ 1) for i in range(cores)])

    piece = shape(snaps, comps, half + 1, rows, span)
    component = shape(snaps, planes, rows, span)
    tiles = max(comps * planes, snaps * planes * rows // ROWS // 2 + 1)
    edge_rows, *pieces = call(
        piece_kernel, "piece", [shape(2, tiles, ROWS, span)] + [piece] * (chips - 1) + [component] * comps
    )(velocity)
    u = pieces[chips - 1 :]
    edge_rows_mate = to_mate(edge_rows)
    u_mate = [to_mate(x) for x in u]
    got = [
        lax.ppermute(piece, "snap", [(i, (i + 2 * k) % cores) for i in range(cores)])
        for k, piece in zip(shifts, pieces[: chips - 1])
    ]

    odd = z % 2 == 1
    levels = max(metric_table.shape[1], rows)
    entries = jnp.pad(row_level[None, :], ((planes, ROWS - 1), (0, levels - rows))).astype(F32)
    table = jnp.pad(metric_table, ((0, ROWS), (0, levels - metric_table.shape[1]))) + entries
    factor = shape(planes, rows, span, dtype=F32)
    metric, volume, operator = call(metric_kernel, "metric", [factor, factor, shape(span, span)])(table)
    scratch = [pltpu.VMEM((half, rows + 2 * ROWS, span), F32)] * 2

    def inner(other, *velocities):
        parts = [shape(snaps, comps, half + 1, rows, span, dtype=F32)] * len(velocities)
        return call(
            functools.partial(inner_kernel, comps, other, len(velocities)),
            "inner",
            parts + [shape(snaps, rows, span, dtype=F32)],
            scratch,
        )(*[x for velocity in velocities for x in velocity], metric, volume, operator)

    part, part_mate, energy = inner(False, u, u_mate)
    mate_planes = half if chips == 2 else planes
    packed = shape(comps * (planes + mate_planes) + 1, ROWS, span)
    first, second = call(functools.partial(pack_kernel, comps, planes, rows), "pack", [packed, packed])(
        table, edge_rows, edge_rows_mate
    )

    def swap(array, first):
        pairs = []
        for i in range(spaces):
            j = ((i - first) ^ 1) + first
            alone = not 0 <= j < spaces
            pairs += [(i * cores + t, i * cores + (t ^ 1) if alone else j * cores + t) for t in range(cores)]
        return lax.ppermute(array, ("space", "snap"), pairs)

    first, second = swap(first, 0), swap(second, 1)
    first, second, part, part_mate, *got = lax.optimization_barrier((first, second, part, part_mate, *got))
    low = jnp.where(z > 0, jnp.where(odd, first, second), 0)
    high = jnp.where(z < spaces - 1, jnp.where(odd, second, first), 0)

    tile = shape(ROWS, span, dtype=F32)
    total, for_mate, back = 0, 0, []
    chip = lax.axis_index("snap") // 2
    *others, energy_other = inner(True, *([u] if chips == 2 else [u, u_mate]))
    for k in shifts:
        parts = part, part_mate
        if k > 1:
            same = (chip < (chip + chips - k) % chips) == (chip < (chip + chips - 1) % chips)
            parts = [jnp.where(same, x, y) for x, y in zip(parts, others)]
        answer = call(
            functools.partial(cross_kernel, k), "cross", [tile] * 3, [pltpu.VMEM((planes, 2, ROWS, span), F32)]
        )(table, *parts, metric, low, high, got[k - 1], *u, *u_mate)
        total = total + answer[0]
        for_mate = for_mate + answer[1]
        back.append(answer[2])
    part_other = others[0]
    w, gain = call(
        edge_kernel,
        "edges",
        [shape(*velocity.shape), shape(snaps, 2, ROWS, span, dtype=F32)],
        [pltpu.VMEM((planes, 2, ROWS, span), F32)],
    )(table, part, part_other, metric, low, high, *u)
    total = total + call(functools.partial(square_kernel, False), "square", tile)(*u, w)
    total = total + call(functools.partial(square_kernel, True), "mates", tile)(*u_mate, w)
    profile = call(functools.partial(profile_kernel, planes), "profile", shape(snaps, rows, dtype=F32))(energy, energy_other, gain)
    for k in shifts:
        total = total + lax.ppermute(back[k - 1], "snap", [(i, (i - 2 * k) % cores) for i in range(cores)])
    total = total + to_mate(for_mate)
    if spaces & (spaces - 1):
        gram = lax.psum(total, "space")
    else:
        gram = total
        step = spaces // 2
        while step:
            gram = gram + lax.ppermute(gram, "space", [(i, i ^ step) for i in range(spaces)])
            step //= 2
    gram = gram[:snaps, : snaps * cores] * (1.0 / (planes * rows * spaces * span))
    return gram, profile


def solution(mesh):
    in_specs = (P(("grp", "snap"), None, None, "space", None), P("space"), P())
    out_specs = (P(("grp", "snap"), None), P(("grp", "snap"), "space"))
    return jax.shard_map(local, mesh=mesh, in_specs=in_specs, out_specs=out_specs, check_vma=False)
```
